32 devices in a mesh: rows: 8 (over z, y), cols: 4 (over x, core).
Axes of the slice: x: 2, y: 2, z: 4, core: 2. Of those that a mesh axis runs over, the one named last changes fastest.
Arguments:
- features: bfloat16 [96, 640, 256], P('rows', 'cols'), may hold values from -6 to 6
- weight: bfloat16 [3, 3, 256, 128], replicated, may hold values from -0.125 to 0.125
- cotangent: bfloat16 [96, 640, 128], P('rows', 'cols'), may hold values from -6 to 6
Outputs:
- conv_out: bfloat16 [96, 640, 128], P('rows', 'cols')
- input_grad: bfloat16 [96, 640, 256], P('rows', 'cols')
- weight_grad: float32 [3, 3, 256, 128], replicated
The draws below stay inside these ranges and needn't reach their ends.
All inputs are finite; a program needn't handle non-finite values.
Results may differ from the reference program's by a relative error of at most 0.001.
Values may be sent and summed in bfloat16 or wider, within the bound.
No kernel may reach another device: no remote copies, remote signals or barrier semaphores. Data moves between devices by JAX's collectives and lax.ppermute only.
A program may use at most 64 MiB of HBM per device.

```python
import jax
import jax.numpy as jnp

CIN = 256
COUT = 128
DILATION_STEP = 12
HEIGHT = 96
WIDTH = 640


def levels(stream_key, extent, pieces, least, largest):
    loudness, own = 1.0, jax.random.fold_in(stream_key, 6)
    for position, parts in pieces:
        draws = jnp.exp(jax.random.uniform(jax.random.fold_in(own, position), (parts,), jnp.float32, least / len(pieces), largest / len(pieces)))
        loudness = loudness * jnp.repeat(draws, extent[position] // parts).reshape([-1 if axis == position else 1 for axis in range(len(extent))])
    return loudness


def normal_values(rng, dims, deviation, most, cuts=(), kind=jnp.bfloat16):
    values = deviation * jax.random.normal(rng, dims, jnp.float32)
    if cuts:
        values = values * levels(rng, dims, cuts, -0.22, 0.18)
    return jnp.clip(values, -most, most).astype(kind)


def setup_inputs(seed: int = 0) -> dict:
    key_of = jax.random.split(jax.random.key(seed), 4)
    features = normal_values(key_of[0], (HEIGHT, WIDTH, CIN), 1.0, 6.0, ((0, 8), (1, 4)))
    weight = normal_values(key_of[1], (3, 3, CIN, COUT), (9 * CIN) ** -0.5, 0.125)
    cotangent = normal_values(key_of[2], (HEIGHT, WIDTH, COUT), 1.0, 6.0, ((0, 8), (1, 4)))
    return {"features": features, "weight": weight, "cotangent": cotangent}


def window(border_padded, row_offset_tap, column_offset_tap, map_height, map_width):
    return border_padded[DILATION_STEP * row_offset_tap:DILATION_STEP * row_offset_tap + map_height, DILATION_STEP * column_offset_tap:DILATION_STEP * column_offset_tap + map_width]

def reference(features, weight, cotangent):
    map_height, map_width = (features.shape[0], features.shape[1])
    cin, cout = (weight.shape[2], weight.shape[3])
    padded_feature_map = jnp.pad(features, ((DILATION_STEP, DILATION_STEP), (DILATION_STEP, DILATION_STEP), (0, 0)))
    padded_gradient_map = jnp.pad(cotangent, ((DILATION_STEP, DILATION_STEP), (DILATION_STEP, DILATION_STEP), (0, 0)))
    flat_grad = cotangent.reshape(map_height * map_width, cout)
    output = jnp.zeros((map_height * map_width, cout), jnp.float32)
    back = jnp.zeros((map_height * map_width, cin), jnp.float32)
    kernels = []
    for row_offset_tap in range(3):
        for column_offset_tap in range(3):
            tap_weight = weight[row_offset_tap, column_offset_tap]
            piece = window(padded_feature_map, row_offset_tap, column_offset_tap, map_height, map_width).reshape(map_height * map_width, cin)
            output = output + jnp.dot(piece, tap_weight, preferred_element_type=jnp.float32)
            gpiece = window(padded_gradient_map, 2 - row_offset_tap, 2 - column_offset_tap, map_height, map_width).reshape(map_height * map_width, cout)
            back = back + jnp.dot(gpiece, tap_weight.T, preferred_element_type=jnp.float32)
            kernels.append(jnp.dot(piece.T, flat_grad, preferred_element_type=jnp.float32))
    scale = 1.0 / jnp.sqrt(jnp.float32(map_height * map_width))
    weight_grad = jnp.stack(kernels).reshape(3, 3, cin, cout) * scale
    conv_out = output.reshape(map_height, map_width, cout).astype(jnp.bfloat16)
    input_grad = back.reshape(map_height, map_width, cin).astype(jnp.bfloat16)
    return (conv_out, input_grad, weight_grad)
```

```python
import jax
import jax.numpy as jnp
from jax import lax
from jax.sharding import Mesh
from jax.sharding import PartitionSpec as P

DILATION_STEP = 12
COLS = ("x", "core")
ALL = ("rows", "x", "core")


def column_extended(cells, width):
    count = lax.axis_size("x") * lax.axis_size("core")
    head = cells[:, :width]
    tail = cells[:, cells.shape[1] - width :]
    left = lax.ppermute(tail, COLS, [(i, i + 1) for i in range(count - 1)])
    right = lax.ppermute(head, COLS, [(i + 1, i) for i in range(count - 1)])
    return left, right


def row_blocks(cells, odd):
    count = lax.axis_size("rows")
    partner = lax.ppermute(cells, "rows", [(i, i ^ 1) for i in range(count)])
    steps = [(i, i - 2 if i % 2 else i + 2) for i in range(count)]
    far = lax.ppermute(partner, "rows", [(i, j) for i, j in steps if 0 <= j < count])
    return partner, far


def stacked(partner, cells, far, odd):
    above = jnp.where(odd, partner, far)
    below = jnp.where(odd, far, partner)
    return jnp.concatenate([above, cells, below], axis=0)


def total(part):
    size = part.shape[0]
    half = size // 2
    core = lax.axis_index("core")
    keep = lax.dynamic_slice_in_dim(part, core * half, half, 0)
    give = lax.dynamic_slice_in_dim(part, (1 - core) * half, half, 0)
    keep = keep + lax.ppermute(give, "core", [(0, 1), (1, 0)])
    chips = lax.axis_size("rows") * lax.axis_size("x")
    pieces = keep.reshape(chips, half // chips, part.shape[1])
    mine = lax.all_to_all(pieces, ("rows", "x"), 0, 0).sum(axis=0)
    own = lax.all_gather(mine, ("rows", "x"), axis=0, tiled=True)
    other = lax.ppermute(own, "core", [(0, 1), (1, 0)])
    first = core == 0
    return jnp.concatenate([jnp.where(first, own, other), jnp.where(first, other, own)], axis=0)


def body(features, weight, cotangent):
    height, width, cin = features.shape
    cout = weight.shape[3]
    pixels = height * width
    step = DILATION_STEP
    odd = lax.axis_index("rows") % 2 == 1

    both = jnp.concatenate([features, cotangent], axis=2)
    left, right = column_extended(both, step)
    grads = jnp.concatenate([left[:, :, cin:], cotangent, right[:, :, cin:]], axis=1)
    cells = jnp.concatenate([left[:, :, :cin], features, right[:, :, :cin]], axis=1)

    grad_map = stacked(*((lambda p: (p[0], grads, p[1]))(row_blocks(grads, odd))), odd)
    flat = features.reshape(pixels, cin)
    kernels = []
    back = jnp.zeros((pixels, cin), jnp.float32)
    windows = []
    for a in range(3):
        for b in range(3):
            piece = grad_map[step * (2 - a) : step * (2 - a) + height, step * (2 - b) : step * (2 - b) + width]
            piece = piece.reshape(pixels, cout)
            windows.append(piece)
            kernels.append(jnp.dot(flat.T, piece, preferred_element_type=jnp.float32))
    part = jnp.stack(kernels).reshape(9 * cin, cout)
    count = pixels
    for axis in ALL:
        count = count * lax.axis_size(axis)
    weight_grad = (total(part) * (1.0 / jnp.sqrt(jnp.float32(count)))).reshape(weight.shape)

    for t in range(9):
        back = back + jnp.dot(windows[t], weight[t // 3, t % 3].T, preferred_element_type=jnp.float32)
    input_grad = back.reshape(height, width, cin).astype(jnp.bfloat16)

    cell_map = stacked(*((lambda p: (p[0], cells, p[1]))(row_blocks(cells, odd))), odd)
    out = jnp.zeros((pixels, cout), jnp.float32)
    for a in range(3):
        for b in range(3):
            piece = cell_map[step * a : step * a + height, step * b : step * b + width].reshape(pixels, cin)
            out = out + jnp.dot(piece, weight[a, b], preferred_element_type=jnp.float32)
    conv_out = out.reshape(height, width, cout).astype(jnp.bfloat16)
    return conv_out, input_grad, weight_grad


def solution(mesh):
    rows, cols = (mesh.shape["rows"], mesh.shape["cols"])
    fine = Mesh(mesh.devices.reshape(rows, cols // 2, 2), ALL)
    placed = P("rows", COLS, None)
    return jax.shard_map(
        body,
        mesh=fine,
        in_specs=(placed, P(), placed),
        out_specs=(placed, placed, P()),
        check_vma=False,
    )
```

```python
import functools
import math

import jax
import jax.numpy as jnp
from jax import lax
from jax.experimental import pallas as pl
from jax.experimental.pallas import tpu as pltpu
from jax.sharding import Mesh
from jax.sharding import PartitionSpec as P

DILATION_STEP = 12
STRIP = 16
TOP = 14
ALL = ("rows", "cols")
VMEM = pltpu.VMEM


def slots(odd):
    return (1 + odd, 2 - odd, 3 * (1 - odd), 3 * odd)


def gather_map(odd, blocks, left, right, ext):
    width = blocks[0].shape[1]
    for place, (block, slot) in enumerate(zip(blocks, slots(odd))):
        ext[slot, :, pl.ds(STRIP, width), :] = block[...]
        ext[slot, :, pl.ds(0, STRIP), :] = left[place]
        ext[slot, :, pl.ds(STRIP + width, STRIP), :] = right[place]


def shift_columns(ext, shifted, width):
    cout = ext.shape[3]
    for slot in range(4):
        whole = ext[slot].astype(jnp.float32)
        for q in range(3):
            start = STRIP + DILATION_STEP * (q - 1)
            shifted[slot, :, :, pl.ds(q * cout, cout)] = whole[:, start : start + width].astype(jnp.bfloat16)


def kernel_grad(chunk, par, f_own, f_par, d_own, d_par, d_near, d_far, left, right, out, ext, shifted, acc):
    odd = par[0]
    half, width, cin = f_par.shape
    cout = d_own.shape[2]
    pixels = half * width
    gather_map(odd, (d_own, d_par, d_near, d_far), left, right, ext)
    shift_columns(ext, shifted, width)
    own, partner = slots(odd)[:2]
    top = jnp.zeros((8, cout), jnp.float32)
    for a in range(3):
        total = None
        for block, slot in ((f_own, own), (f_par, partner)):
            lhs = block[...].reshape(pixels, cin)
            rhs = shifted[slot + 1 - a].reshape(pixels, 3 * cout)
            term = lax.dot_general(lhs, rhs, (((0,), (0,)), ((), ())), preferred_element_type=jnp.float32)
            total = term if total is None else total + term
        for b in range(3):
            piece = total[:, (2 - b) * cout : (3 - b) * cout]
            acc[pl.ds((3 * a + b) * cin, cin), :] = piece
            top = jnp.maximum(top, jnp.max(jnp.abs(piece).reshape(cin // 8, 8, cout), axis=0))
    most = jnp.max(jnp.max(top, axis=0, keepdims=True), axis=1, keepdims=True)
    level = jnp.ceil(jnp.log2(jnp.maximum(jnp.broadcast_to(most, (8, cout)), 2.0**-110)))
    scale = jnp.exp2(TOP - level)[:1]
    for c in range(out.shape[0]):
        out[c, pl.ds(0, chunk), :] = acc[pl.ds(c * chunk, chunk), :] * scale
        out[c, pl.ds(chunk, out.shape[1] - chunk), :] = jnp.broadcast_to(level[:1], (out.shape[1] - chunk, cout))


def kernel_back(par, w, d_own, d_par, d_near, d_far, left, right, out_own, out_par, ext, shifted):
    odd = par[0]
    half, width, cout = d_own.shape
    cin = w.shape[2]
    pixels = half * width
    gather_map(odd, (d_own, d_par, d_near, d_far), left, right, ext)
    shift_columns(ext, shifted, width)
    own, partner = slots(odd)[:2]
    for out, slot in ((out_own, own), (out_par, partner)):
        total = None
        for a in range(3):
            lhs = shifted[slot + 1 - a].reshape(pixels, 3 * cout)
            rhs = jnp.concatenate([w[a, 2 - q] for q in range(3)], axis=1)
            term = lax.dot_general(lhs, rhs, (((1,), (1,)), ((), ())), preferred_element_type=jnp.float32)
            total = term if total is None else total + term
        out[...] = total.astype(jnp.bfloat16).reshape(half, width, cin)


def kernel_out(par, w, f_own, f_par, f_near, f_far, left, right, out_own, out_par, ext):
    odd = par[0]
    half, width, cin = f_own.shape
    cout = w.shape[3]
    wide = width + 2 * STRIP
    gather_map(odd, (f_own, f_par, f_near, f_far), left, right, ext)
    own, partner = slots(odd)[:2]
    for out, slot in ((out_own, own), (out_par, partner)):
        total = None
        for a in range(3):
            lhs = ext[slot + a - 1].reshape(half * wide, cin)
            rhs = jnp.concatenate([w[a, b] for b in range(3)], axis=1)
            term = jnp.dot(lhs, rhs, preferred_element_type=jnp.float32)
            total = term if total is None else total + term
        total = total.reshape(half, wide, 3 * cout)
        result = None
        for b in range(3):
            start = STRIP + DILATION_STEP * (b - 1)
            term = total[:, start : start + width, b * cout : (b + 1) * cout]
            result = term if result is None else result + term
        out[...] = result.astype(jnp.bfloat16)


def call(kernel, operands, outs, scratch, flops):
    whole = pl.BlockSpec(memory_space=VMEM)
    size = sum(x.size * x.dtype.itemsize for x in operands) + sum(math.prod(o.shape) * o.dtype.itemsize for o in outs)
    return pl.pallas_call(
        kernel,
        out_shape=outs,
        in_specs=[pl.BlockSpec(memory_space=pltpu.SMEM)] + [whole] * (len(operands) - 1),
        out_specs=[whole] * len(outs),
        scratch_shapes=scratch,
        compiler_params=pltpu.CompilerParams(vmem_limit_bytes=48 * 1024 * 1024),
        cost_estimate=pl.CostEstimate(flops=flops, bytes_accessed=size, transcendentals=0),
    )(*operands)


def strips(blocks, count):
    width = blocks[0].shape[1]
    tails = jnp.stack([x[:, width - STRIP :] for x in blocks])
    heads = jnp.stack([x[:, :STRIP] for x in blocks])
    left = lax.ppermute(tails, "cols", [(i, i + 1) for i in range(count - 1)])
    right = lax.ppermute(heads, "cols", [(i + 1, i) for i in range(count - 1)])
    return left, right


def joined(odd, own, other):
    low = jnp.where(odd == 1, other, own)
    high = jnp.where(odd == 1, own, other)
    return jnp.concatenate([low, high], axis=0)


def body(features, weight, cotangent):
    height, width, cin = features.shape
    cout = weight.shape[3]
    half = height // 2
    rows, cols = (lax.axis_size("rows"), lax.axis_size("cols"))
    devices = rows * cols
    odd = lax.axis_index("rows") % 2
    par = odd.astype(jnp.int32).reshape(1)

    swap = [(i, i ^ 1) for i in range(rows)]
    up = [(i, i + 2 if i % 2 else i - 2) for i in range(rows)]
    near = [(i, j) for i, j in up if 0 <= j < rows]
    far = [(j, i) for i, j in near]

    def pick(cells, which):
        return lax.dynamic_slice_in_dim(cells, which * half, half, 0)

    d_own, d_give = (pick(cotangent, odd), pick(cotangent, 1 - odd))
    f_own, f_give = (pick(features, odd), pick(features, 1 - odd))
    d_par = lax.ppermute(d_give, "rows", swap)
    d_near = lax.ppermute(d_own, "rows", near)
    f_par = lax.ppermute(f_give, "rows", swap)
    f_near = lax.ppermute(f_own, "rows", near)
    d_far = lax.ppermute(d_par, "rows", far)
    d_blocks = (d_own, d_par, d_near, d_far)
    d_left, d_right = strips(d_blocks, cols)

    wide = width + 2 * STRIP
    chunk = 9 * cin // devices
    deep = -(-(chunk + 1) // STRIP) * STRIP
    flops = 2 * 9 * height * width * cin * cout
    ext = VMEM((4, half, wide, cout), jnp.bfloat16)
    shifted = VMEM((4, half, width, 3 * cout), jnp.bfloat16)
    (scaled,) = call(
        functools.partial(kernel_grad, chunk),
        (par, f_own, f_par) + d_blocks + (d_left, d_right),
        [jax.ShapeDtypeStruct((devices, deep, cout), jnp.float32)],
        [ext, shifted, VMEM((9 * cin, cout), jnp.float32)],
        flops,
    )
    got = lax.all_to_all(scaled.astype(jnp.float16), ALL, 0, 0)

    half_grad = jax.ShapeDtypeStruct((half, width, cin), jnp.bfloat16)
    g_own, g_par = call(
        kernel_back, (par, weight) + d_blocks + (d_left, d_right), [half_grad, half_grad], [ext, shifted], flops
    )
    g_other = lax.ppermute(g_par, "rows", swap)

    f_far = lax.ppermute(f_par, "rows", far)
    f_blocks = (f_own, f_par, f_near, f_far)
    f_left, f_right = strips(f_blocks, cols)

    levels = got[:, chunk, 0].astype(jnp.float32)
    highest = jnp.max(levels)
    shares = got[:, :chunk].astype(jnp.float32) * jnp.exp2(levels - highest)[:, None, None]
    mine = (jnp.sum(shares, axis=0) * (1.0 / devices)).astype(jnp.float16)
    spread = lax.all_to_all(jnp.broadcast_to(mine, (devices, chunk, cout)), ALL, 0, 0)

    half_out = jax.ShapeDtypeStruct((half, width, cout), jnp.bfloat16)
    o_own, o_par = call(
        kernel_out,
        (par, weight) + f_blocks + (f_left, f_right),
        [half_out, half_out],
        [VMEM((4, half, wide, cin), jnp.bfloat16)],
        flops,
    )
    o_other = lax.ppermute(o_par, "rows", swap)

    norm = devices / jnp.sqrt(jnp.float32(height * width * devices))
    weight_grad = spread.astype(jnp.float32) * (jnp.exp2(highest - TOP) * norm)
    return (
        joined(odd, o_own, o_other),
        joined(odd, g_own, g_other),
        weight_grad.reshape(weight.shape),
    )


def solution(mesh):
    placed = P("rows", "cols", None)
    return jax.shard_map(
        body,
        mesh=mesh,
        in_specs=(placed, P(), placed),
        out_specs=(placed, placed, P()),
        check_vma=False,
    )
```

```python
import functools
import math

import jax
import jax.numpy as jnp
from jax import lax
from jax.experimental import pallas as pl
from jax.experimental.pallas import tpu as pltpu
from jax.sharding import Mesh
from jax.sharding import PartitionSpec as P

DILATION_STEP = 12
STRIP = 16
TOP = 14
ALL = ("rows", "cols")
VMEM = pltpu.VMEM


def slots(odd):
    return (1 + odd, 2 - odd, 3 * (1 - odd), 3 * odd)


def gather_map(odd, blocks, left, right, ext):
    width = blocks[0].shape[1]
    for place, (block, slot) in enumerate(zip(blocks, slots(odd))):
        ext[slot, :, pl.ds(STRIP, width), :] = block[...]
        ext[slot, :, pl.ds(0, STRIP), :] = left[place]
        ext[slot, :, pl.ds(STRIP + width, STRIP), :] = right[place]


def shift_columns(ext, shifted, width):
    cout = ext.shape[3]
    for slot in range(4):
        whole = ext[slot].astype(jnp.float32)
        for q in range(3):
            start = STRIP + DILATION_STEP * (q - 1)
            shifted[slot, :, :, pl.ds(q * cout, cout)] = whole[:, start : start + width].astype(jnp.bfloat16)


def kernel_extend(par, cells, left, right, own, give):
    odd = par[0]
    half, wide, _ = own.shape
    width = cells.shape[1]
    for out, start in ((own, odd * half), (give, (1 - odd) * half)):
        rows = pl.ds(start, half)
        out[:, pl.ds(0, STRIP), :] = left[rows]
        out[:, pl.ds(STRIP, width), :] = cells[rows]
        out[:, pl.ds(STRIP + width, STRIP), :] = right[rows]


def kernel_grad(chunk, par, f_own, f_par, d_own, d_par, d_near, d_far, out, ext, shifted, acc):
    odd = par[0]
    half, width, cout = d_own.shape
    cin = f_own.shape[2]
    pixels = half * width
    for block, slot in zip((d_own, d_par, d_near, d_far), slots(odd)):
        ext[slot] = block[...]
    own, partner = slots(odd)[:2]
    total = None
    for block, slot in ((f_own, own), (f_par, partner)):
        whole = block[...].astype(jnp.float32)
        for b in range(3):
            start = STRIP + DILATION_STEP * (b - 1)
            shifted[:, :, pl.ds(b * cin, cin)] = whole[:, start : start + width].astype(jnp.bfloat16)
        lhs = shifted[...].reshape(pixels, 3 * cin)
        rhs = jnp.concatenate([ext[slot + 1 - a].reshape(pixels, cout) for a in range(3)], axis=1)
        term = lax.dot_general(lhs, rhs, (((0,), (0,)), ((), ())), preferred_element_type=jnp.float32)
        total = term if total is None else total + term
    top = jnp.zeros((8, cout), jnp.float32)
    for a in range(3):
        for b in range(3):
            piece = total[b * cin : (b + 1) * cin, a * cout : (a + 1) * cout]
            acc[pl.ds((3 * a + b) * cin, cin), :] = piece
            top = jnp.maximum(top, jnp.max(jnp.abs(piece).reshape(cin // 8, 8, cout), axis=0))
    most = jnp.max(jnp.max(top, axis=0, keepdims=True), axis=1, keepdims=True)
    level = jnp.ceil(jnp.log2(jnp.maximum(jnp.broadcast_to(most, (8, cout)), 2.0**-110)))
    scale = jnp.exp2(TOP - level)[:1]
    for c in range(out.shape[0]):
        out[c, pl.ds(0, chunk), :] = acc[pl.ds(c * chunk, chunk), :] * scale
        out[c, pl.ds(chunk, out.shape[1] - chunk), :] = jnp.broadcast_to(level[:1], (out.shape[1] - chunk, cout))


def kernel_back(par, w, d_own, d_par, d_near, d_far, left, right, out_own, out_par, ext, shifted):
    odd = par[0]
    half, width, cout = d_own.shape
    cin = w.shape[2]
    pixels = half * width
    gather_map(odd, (d_own, d_par, d_near, d_far), left, right, ext)
    shift_columns(ext, shifted, width)
    own, partner = slots(odd)[:2]
    for out, slot in ((out_own, own), (out_par, partner)):
        total = None
        for a in range(3):
            lhs = shifted[slot + 1 - a].reshape(pixels, 3 * cout)
            rhs = jnp.concatenate([w[a, 2 - q] for q in range(3)], axis=1)
            term = lax.dot_general(lhs, rhs, (((1,), (1,)), ((), ())), preferred_element_type=jnp.float32)
            total = term if total is None else total + term
        out[...] = total.astype(jnp.bfloat16).reshape(half, width, cin)


def kernel_out(par, w, f_own, f_par, f_near, f_far, out_own, out_par, ext):
    odd = par[0]
    half, width, cout = out_own.shape
    wide, cin = f_own.shape[1:]
    for block, slot in zip((f_own, f_par, f_near, f_far), slots(odd)):
        ext[slot] = block[...]
    own, partner = slots(odd)[:2]
    for out, slot in ((out_own, own), (out_par, partner)):
        total = None
        for a in range(3):
            lhs = ext[slot + a - 1].reshape(half * wide, cin)
            rhs = jnp.concatenate([w[a, b] for b in range(3)], axis=1)
            term = jnp.dot(lhs, rhs, preferred_element_type=jnp.float32)
            total = term if total is None else total + term
        total = total.reshape(half, wide, 3 * cout)
        result = None
        for b in range(3):
            start = STRIP + DILATION_STEP * (b - 1)
            term = total[:, start : start + width, b * cout : (b + 1) * cout]
            result = term if result is None else result + term
        out[...] = result.astype(jnp.bfloat16)


def call(kernel, operands, outs, scratch, flops):
    whole = pl.BlockSpec(memory_space=VMEM)
    size = sum(x.size * x.dtype.itemsize for x in operands) + sum(math.prod(o.shape) * o.dtype.itemsize for o in outs)
    return pl.pallas_call(
        kernel,
        out_shape=outs,
        in_specs=[pl.BlockSpec(memory_space=pltpu.SMEM)] + [whole] * (len(operands) - 1),
        out_specs=[whole] * len(outs),
        scratch_shapes=scratch,
        compiler_params=pltpu.CompilerParams(vmem_limit_bytes=48 * 1024 * 1024),
        cost_estimate=pl.CostEstimate(flops=flops, bytes_accessed=size, transcendentals=0),
    )(*operands)


def strips(blocks, count):
    width = blocks[0].shape[-2]
    tails = [x[..., width - STRIP :, :] for x in blocks]
    heads = [x[..., :STRIP, :] for x in blocks]
    tails, heads = (x[0] if len(x) == 1 else jnp.stack(x) for x in (tails, heads))
    left = lax.ppermute(tails, "cols", [(i, i + 1) for i in range(count - 1)])
    right = lax.ppermute(heads, "cols", [(i + 1, i) for i in range(count - 1)])
    return left, right


def joined(odd, own, other):
    low = jnp.where(odd == 1, other, own)
    high = jnp.where(odd == 1, own, other)
    return jnp.concatenate([low, high], axis=0)


def body(features, weight, cotangent):
    height, width, cin = features.shape
    cout = weight.shape[3]
    half = height // 2
    rows, cols = (lax.axis_size("rows"), lax.axis_size("cols"))
    devices = rows * cols
    odd = lax.axis_index("rows") % 2
    par = odd.astype(jnp.int32).reshape(1)

    swap = [(i, i ^ 1) for i in range(rows)]
    up = [(i, i + 2 if i % 2 else i - 2) for i in range(rows)]
    near = [(i, j) for i, j in up if 0 <= j < rows]
    far = [(j, i) for i, j in near]

    def pick(cells, which):
        return lax.dynamic_slice_in_dim(cells, which * half, half, 0)

    wide = width + 2 * STRIP
    chunk = 9 * cin // devices
    deep = -(-(chunk + 1) // STRIP) * STRIP
    flops = 2 * 9 * height * width * cin * cout

    d_own, d_give = (pick(cotangent, odd), pick(cotangent, 1 - odd))
    d_par = lax.ppermute(d_give, "rows", swap)
    f_left, f_right = strips((features,), cols)
    d_near = lax.ppermute(d_own, "rows", near)
    broad = jax.ShapeDtypeStruct((half, wide, cin), jnp.bfloat16)
    f_own, f_give = call(kernel_extend, (par, features, f_left, f_right), [broad, broad], [], 0)
    f_par = lax.ppermute(f_give, "rows", swap)
    f_near = lax.ppermute(f_own, "rows", near)
    d_far = lax.ppermute(d_par, "rows", far)
    f_far = lax.ppermute(f_par, "rows", far)
    d_blocks = (d_own, d_par, d_near, d_far)

    f_own, f_near = lax.optimization_barrier((f_own, f_near))
    ext = VMEM((4, half, wide, cout), jnp.bfloat16)
    (scaled,) = call(
        functools.partial(kernel_grad, chunk),
        (par, f_own, f_par) + d_blocks,
        [jax.ShapeDtypeStruct((devices, deep, cout), jnp.float32)],
        [
            VMEM((4, half, width, cout), jnp.bfloat16),
            VMEM((half, width, 3 * cin), jnp.bfloat16),
            VMEM((9 * cin, cout), jnp.float32),
        ],
        flops,
    )
    got = lax.all_to_all(scaled.astype(jnp.float16), ALL, 0, 0)

    d_left, d_right = strips(d_blocks, cols)
    d_left, f_far = lax.optimization_barrier((d_left, f_far))
    half_grad = jax.ShapeDtypeStruct((half, width, cin), jnp.bfloat16)
    g_own, g_par = call(
        kernel_back,
        (par, weight) + d_blocks + (d_left, d_right),
        [half_grad, half_grad],
        [ext, VMEM((4, half, width, 3 * cout), jnp.bfloat16)],
        flops,
    )
    g_other = lax.ppermute(g_par, "rows", swap)

    half_out = jax.ShapeDtypeStruct((half, width, cout), jnp.bfloat16)
    o_own, o_par = call(
        kernel_out,
        (par, weight, f_own, f_par, f_near, f_far),
        [half_out, half_out],
        [VMEM((4, half, wide, cin), jnp.bfloat16)],
        flops,
    )
    o_other = lax.ppermute(o_par, "rows", swap)

    levels = got[:, chunk : chunk + 1].astype(jnp.float32)
    highest = jnp.max(levels, axis=0, keepdims=True)
    shares = got[:, :chunk].astype(jnp.float32) * jnp.exp2(levels - highest)
    mine = (jnp.sum(shares, axis=0, keepdims=True) * (1.0 / devices)).astype(jnp.float16)
    spread = lax.all_to_all(jnp.broadcast_to(mine, (devices, chunk, cout)), ALL, 0, 0)

    norm = devices / jnp.sqrt(jnp.float32(height * width * devices))
    weight_grad = spread.astype(jnp.float32) * (jnp.exp2(highest - TOP) * norm)
    return (
        joined(odd, o_own, o_other),
        joined(odd, g_own, g_other),
        weight_grad.reshape(weight.shape),
    )


def solution(mesh):
    placed = P("rows", "cols", None)
    return jax.shard_map(
        body,
        mesh=mesh,
        in_specs=(placed, P(), placed),
        out_specs=(placed, placed, P()),
        check_vma=False,
    )
```

```python
import functools
import math

import jax
import jax.numpy as jnp
from jax import lax
from jax.experimental import pallas as pl
from jax.experimental.pallas import tpu as pltpu
from jax.sharding import Mesh
from jax.sharding import PartitionSpec as P

DILATION_STEP = 12
STRIP = 16
TOP = 14
COLS = ("x", "core")
CHIPS = ("rows", "x")
VMEM = pltpu.VMEM


def slots(odd):
    return (1 + odd, 2 - odd, 3 * (1 - odd), 3 * odd)


def gather_map(odd, blocks, left, right, ext):
    width = blocks[0].shape[1]
    for place, (block, slot) in enumerate(zip(blocks, slots(odd))):
        ext[slot, :, pl.ds(STRIP, width), :] = block[...]
        ext[slot, :, pl.ds(0, STRIP), :] = left[place]
        ext[slot, :, pl.ds(STRIP + width, STRIP), :] = right[place]


def shift_columns(ext, shifted, width):
    cout = ext.shape[3]
    for slot in range(4):
        whole = ext[slot].astype(jnp.float32)
        for q in range(3):
            start = STRIP + DILATION_STEP * (q - 1)
            shifted[slot, :, :, pl.ds(q * cout, cout)] = whole[:, start : start + width].astype(jnp.bfloat16)


def kernel_extend(par, cells, left, right, own, give):
    odd = par[0]
    half, wide, _ = own.shape
    width = cells.shape[1]
    for out, start in ((own, odd * half), (give, (1 - odd) * half)):
        rows = pl.ds(start, half)
        out[:, pl.ds(0, STRIP), :] = left[rows]
        out[:, pl.ds(STRIP, width), :] = cells[rows]
        out[:, pl.ds(STRIP + width, STRIP), :] = right[rows]


def kernel_grad(par, f_own, f_par, d_own, d_par, d_near, d_far, keep, give, ext, shifted, acc):
    odd, core = (par[0], par[1])
    half, width, cout = d_own.shape
    cin = f_own.shape[2]
    pixels = half * width
    for block, slot in zip((d_own, d_par, d_near, d_far), slots(odd)):
        ext[slot] = block[...]
    own, partner = slots(odd)[:2]
    total = None
    for block, slot in ((f_own, own), (f_par, partner)):
        whole = block[...].astype(jnp.float32)
        for b in range(3):
            start = STRIP + DILATION_STEP * (b - 1)
            shifted[:, :, pl.ds(b * cin, cin)] = whole[:, start : start + width].astype(jnp.bfloat16)
        lhs = shifted[...].reshape(pixels, 3 * cin)
        rhs = jnp.concatenate([ext[slot + 1 - a].reshape(pixels, cout) for a in range(3)], axis=1)
        term = lax.dot_general(lhs, rhs, (((0,), (0,)), ((), ())), preferred_element_type=jnp.float32)
        total = term if total is None else total + term
    for a in range(3):
        for b in range(3):
            piece = total[b * cin : (b + 1) * cin, a * cout : (a + 1) * cout]
            acc[pl.ds((3 * a + b) * cin, cin), :] = piece
    size = keep.shape[0]
    keep[...] = acc[pl.ds(core * size, size), :]
    give[...] = acc[pl.ds((1 - core) * size, size), :]


def kernel_scale(chunk, par, keep, given, out):
    total = keep[...] + given[...]
    size, cout = keep.shape
    top = jnp.max(jnp.abs(total).reshape(size // 8, 8, cout), axis=0)
    most = jnp.max(jnp.max(top, axis=0, keepdims=True), axis=1, keepdims=True)
    level = jnp.ceil(jnp.log2(jnp.maximum(jnp.broadcast_to(most, (8, cout)), 2.0**-110)))
    scaled = total * jnp.exp2(TOP - level)[:1]
    for c in range(out.shape[0]):
        out[c, pl.ds(0, chunk), :] = scaled[c * chunk : (c + 1) * chunk]
        out[c, pl.ds(chunk, out.shape[1] - chunk), :] = jnp.broadcast_to(level[:1], (out.shape[1] - chunk, cout))


def kernel_back(par, w, d_own, d_par, d_near, d_far, left, right, out_own, out_par, ext, shifted):
    odd = par[0]
    half, width, cout = d_own.shape
    cin = w.shape[2]
    pixels = half * width
    gather_map(odd, (d_own, d_par, d_near, d_far), left, right, ext)
    shift_columns(ext, shifted, width)
    own, partner = slots(odd)[:2]
    for out, slot in ((out_own, own), (out_par, partner)):
        total = None
        for a in range(3):
            lhs = shifted[slot + 1 - a].reshape(pixels, 3 * cout)
            rhs = jnp.concatenate([w[a, 2 - q] for q in range(3)], axis=1)
            term = lax.dot_general(lhs, rhs, (((1,), (1,)), ((), ())), preferred_element_type=jnp.float32)
            total = term if total is None else total + term
        out[...] = total.astype(jnp.bfloat16).reshape(half, width, cin)


def kernel_out(par, w, f_own, f_par, f_near, f_far, out_own, out_par, ext):
    odd = par[0]
    half, width, cout = out_own.shape
    wide, cin = f_own.shape[1:]
    for block, slot in zip((f_own, f_par, f_near, f_far), slots(odd)):
        ext[slot] = block[...]
    own, partner = slots(odd)[:2]
    for out, slot in ((out_own, own), (out_par, partner)):
        total = None
        for a in range(3):
            lhs = ext[slot + a - 1].reshape(half * wide, cin)
            rhs = jnp.concatenate([w[a, b] for b in range(3)], axis=1)
            term = jnp.dot(lhs, rhs, preferred_element_type=jnp.float32)
            total = term if total is None else total + term
        total = total.reshape(half, wide, 3 * cout)
        result = None
        for b in range(3):
            start = STRIP + DILATION_STEP * (b - 1)
            term = total[:, start : start + width, b * cout : (b + 1) * cout]
            result = term if result is None else result + term
        out[...] = result.astype(jnp.bfloat16)


def call(kernel, operands, outs, scratch, flops):
    whole = pl.BlockSpec(memory_space=VMEM)
    size = sum(x.size * x.dtype.itemsize for x in operands) + sum(math.prod(o.shape) * o.dtype.itemsize for o in outs)
    return pl.pallas_call(
        kernel,
        out_shape=outs,
        in_specs=[pl.BlockSpec(memory_space=pltpu.SMEM)] + [whole] * (len(operands) - 1),
        out_specs=[whole] * len(outs),
        scratch_shapes=scratch,
        compiler_params=pltpu.CompilerParams(vmem_limit_bytes=48 * 1024 * 1024),
        cost_estimate=pl.CostEstimate(flops=flops, bytes_accessed=size, transcendentals=0),
    )(*operands)


def strips(blocks, count):
    width = blocks[0].shape[-2]
    tails = [x[..., width - STRIP :, :] for x in blocks]
    heads = [x[..., :STRIP, :] for x in blocks]
    tails, heads = (x[0] if len(x) == 1 else jnp.stack(x) for x in (tails, heads))
    left = lax.ppermute(tails, COLS, [(i, i + 1) for i in range(count - 1)])
    right = lax.ppermute(heads, COLS, [(i + 1, i) for i in range(count - 1)])
    return left, right


def joined(odd, own, other):
    low = jnp.where(odd == 1, other, own)
    high = jnp.where(odd == 1, own, other)
    return jnp.concatenate([low, high], axis=0)


def body(features, weight, cotangent):
    height, width, cin = features.shape
    cout = weight.shape[3]
    half = height // 2
    rows = lax.axis_size("rows")
    cols = lax.axis_size("x") * lax.axis_size("core")
    chips = rows * lax.axis_size("x")
    odd = lax.axis_index("rows") % 2
    core = lax.axis_index("core")
    par = jnp.stack([odd, core]).astype(jnp.int32)

    swap = [(i, i ^ 1) for i in range(rows)]
    other_core = [(0, 1), (1, 0)]
    up = [(i, i + 2 if i % 2 else i - 2) for i in range(rows)]
    near = [(i, j) for i, j in up if 0 <= j < rows]
    far = [(j, i) for i, j in near]
    fence = lax.optimization_barrier

    def pick(cells, which):
        return lax.dynamic_slice_in_dim(cells, which * half, half, 0)

    wide = width + 2 * STRIP
    share = 9 * cin // 2
    chunk = share // chips
    deep = -(-(chunk + 1) // STRIP) * STRIP
    flops = 2 * 9 * height * width * cin * cout

    d_own, d_give = (pick(cotangent, odd), pick(cotangent, 1 - odd))
    d_par = lax.ppermute(d_give, "rows", swap)
    f_left, f_right = strips((features,), cols)
    d_near = lax.ppermute(d_own, "rows", near)
    broad = jax.ShapeDtypeStruct((half, wide, cin), jnp.bfloat16)
    f_own, f_give = call(kernel_extend, (par, features, f_left, f_right), [broad, broad], [], 0)
    f_give, d_par = fence((f_give, d_par))
    d_far = lax.ppermute(d_par, "rows", far)
    f_par = lax.ppermute(f_give, "rows", swap)
    f_near = lax.ppermute(f_own, "rows", near)
    f_far = lax.ppermute(f_par, "rows", far)
    d_blocks = (d_own, d_par, d_near, d_far)
    d_left, d_right = strips(d_blocks, cols)

    f_own, f_near = fence((f_own, f_near))
    part = jax.ShapeDtypeStruct((share, cout), jnp.float32)
    keep, give = call(
        kernel_grad,
        (par, f_own, f_par) + d_blocks,
        [part, part],
        [
            VMEM((4, half, width, cout), jnp.bfloat16),
            VMEM((half, width, 3 * cin), jnp.bfloat16),
            VMEM((9 * cin, cout), jnp.float32),
        ],
        flops,
    )
    given = lax.ppermute(give, "core", other_core)

    half_grad = jax.ShapeDtypeStruct((half, width, cin), jnp.bfloat16)
    g_own, g_par = call(
        kernel_back,
        (par, weight) + d_blocks + (d_left, d_right),
        [half_grad, half_grad],
        [VMEM((4, half, wide, cout), jnp.bfloat16), VMEM((4, half, width, 3 * cout), jnp.bfloat16)],
        flops,
    )
    given, g_par = fence((given, g_par))
    g_other = lax.ppermute(g_par, "rows", swap)

    (scaled,) = call(
        functools.partial(kernel_scale, chunk),
        (par, keep, given),
        [jax.ShapeDtypeStruct((chips, deep, cout), jnp.float32)],
        [],
        0,
    )
    scaled, f_far = fence((scaled.astype(jnp.float16), f_far))
    got = lax.all_to_all(scaled, CHIPS, 0, 0)

    half_out = jax.ShapeDtypeStruct((half, width, cout), jnp.bfloat16)
    o_own, o_par = call(
        kernel_out,
        (par, weight, f_own, f_par, f_near, f_far),
        [half_out, half_out],
        [VMEM((4, half, wide, cin), jnp.bfloat16)],
        flops,
    )
    got, o_par = fence((got, o_par))
    o_other = lax.ppermute(o_par, "rows", swap)

    levels = got[:, chunk : chunk + 1].astype(jnp.float32)
    highest = jnp.max(levels, axis=0, keepdims=True)
    shares = got.astype(jnp.float32) * jnp.exp2(levels - highest)
    mine = jnp.sum(shares, axis=0, keepdims=True) * (1.0 / chips)
    place = lax.broadcasted_iota(jnp.int32, mine.shape, 1)
    mine = jnp.where(place < chunk, mine, highest).astype(jnp.float16)
    spread = lax.all_to_all(jnp.broadcast_to(mine, (chips, deep, cout)), CHIPS, 0, 0)
    other = lax.ppermute(spread, "core", other_core)

    norm = chips / jnp.sqrt(jnp.float32(height * width * chips * 2))

    def restored(low, high):
        picked = jnp.where(core == 0, low, high)
        factor = jnp.exp2(picked[:1, chunk : chunk + 1].astype(jnp.float32) - TOP) * norm
        return (picked[:, :chunk].astype(jnp.float32) * factor).reshape(share, cout)

    weight_grad = jnp.concatenate([restored(spread, other), restored(other, spread)], axis=0)
    return (
        joined(odd, o_own, o_other),
        joined(odd, g_own, g_other),
        weight_grad.reshape(weight.shape),
    )


def solution(mesh):
    rows, cols = (mesh.shape["rows"], mesh.shape["cols"])
    fine = Mesh(mesh.devices.reshape(rows, cols // 2, 2), ("rows",) + COLS)
    placed = P("rows", COLS, None)
    return jax.shard_map(
        body,
        mesh=fine,
        in_specs=(placed, P(), placed),
        out_specs=(placed, placed, P()),
        check_vma=False,
    )
```

```python
import functools
import math

import jax
import jax.numpy as jnp
from jax import lax
from jax.experimental import pallas as pl
from jax.experimental.pallas import tpu as pltpu
from jax.sharding import Mesh
from jax.sharding import PartitionSpec as P

DILATION_STEP = 12
STRIP = 16
TOP = 14
COLS = ("x", "core")
CHIPS = ("rows", "x")
VMEM = pltpu.VMEM


def slots(odd):
    return (1 + odd, 2 - odd, 3 * (1 - odd), 3 * odd)


def gather_map(odd, blocks, left, right, ext):
    width = blocks[0].shape[1]
    for place, (block, slot) in enumerate(zip(blocks, slots(odd))):
        ext[slot, :, pl.ds(STRIP, width), :] = block[...]
        ext[slot, :, pl.ds(0, STRIP), :] = left[place]
        ext[slot, :, pl.ds(STRIP + width, STRIP), :] = right[place]


def shift_columns(ext, shifted, width):
    cout = ext.shape[3]
    for slot in range(4):
        whole = ext[slot].astype(jnp.float32)
        for q in range(3):
            start = STRIP + DILATION_STEP * (q - 1)
            shifted[slot, :, :, pl.ds(q * cout, cout)] = whole[:, start : start + width].astype(jnp.bfloat16)


def kernel_grad(par, f_own, f_par, d_own, d_par, d_near, d_far, left, right, keep, give, ext, shifted, acc):
    odd, core = (par[0], par[1])
    half, width, cout = d_own.shape
    cin = f_own.shape[2]
    pixels = half * width
    gather_map(odd, (d_own, d_par, d_near, d_far), left, right, ext)
    shift_columns(ext, shifted, width)
    own, partner = slots(odd)[:2]
    total = None
    for block, slot in ((f_own, own), (f_par, partner)):
        lhs = block[...].reshape(pixels, cin)
        rhs = jnp.concatenate([shifted[slot + 1 - a].reshape(pixels, 3 * cout) for a in range(3)], axis=1)
        term = lax.dot_general(lhs, rhs, (((0,), (0,)), ((), ())), preferred_element_type=jnp.float32)
        total = term if total is None else total + term
    for a in range(3):
        for b in range(3):
            start = (3 * a + 2 - b) * cout
            acc[pl.ds((3 * a + b) * cin, cin), :] = total[:, start : start + cout]
    size = keep.shape[0]
    keep[...] = acc[pl.ds(core * size, size), :]
    give[...] = acc[pl.ds((1 - core) * size, size), :]


def kernel_scale(chunk, par, keep, given, out):
    total = keep[...] + given[...]
    size, cout = keep.shape
    top = jnp.max(jnp.abs(total).reshape(size // 8, 8, cout), axis=0)
    most = jnp.max(jnp.max(top, axis=0, keepdims=True), axis=1, keepdims=True)
    level = jnp.ceil(jnp.log2(jnp.maximum(jnp.broadcast_to(most, (8, cout)), 2.0**-110)))
    scaled = total * jnp.exp2(TOP - level)[:1]
    for c in range(out.shape[0]):
        out[c, pl.ds(0, chunk), :] = scaled[c * chunk : (c + 1) * chunk]
        out[c, pl.ds(chunk, out.shape[1] - chunk), :] = jnp.broadcast_to(level[:1], (out.shape[1] - chunk, cout))


def kernel_back(par, w, d_own, d_par, d_near, d_far, left, right, out_own, out_par, ext, shifted):
    odd = par[0]
    half, width, cout = d_own.shape
    cin = w.shape[2]
    pixels = half * width
    gather_map(odd, (d_own, d_par, d_near, d_far), left, right, ext)
    shift_columns(ext, shifted, width)
    own, partner = slots(odd)[:2]
    for out, slot in ((out_own, own), (out_par, partner)):
        total = None
        for a in range(3):
            lhs = shifted[slot + 1 - a].reshape(pixels, 3 * cout)
            rhs = jnp.concatenate([w[a, 2 - q] for q in range(3)], axis=1)
            term = lax.dot_general(lhs, rhs, (((1,), (1,)), ((), ())), preferred_element_type=jnp.float32)
            total = term if total is None else total + term
        out[...] = total.astype(jnp.bfloat16).reshape(half, width, cin)


def kernel_out(par, w, f_own, f_par, f_near, f_far, left, right, out_own, out_par, ext):
    odd = par[0]
    half, width, cout = out_own.shape
    cin = f_own.shape[2]
    wide = width + 2 * STRIP
    gather_map(odd, (f_own, f_par, f_near, f_far), left, right, ext)
    own, partner = slots(odd)[:2]
    for out, slot in ((out_own, own), (out_par, partner)):
        total = None
        for a in range(3):
            lhs = ext[slot + a - 1].reshape(half * wide, cin)
            rhs = jnp.concatenate([w[a, b] for b in range(3)], axis=1)
            term = jnp.dot(lhs, rhs, preferred_element_type=jnp.float32)
            total = term if total is None else total + term
        total = total.reshape(half, wide, 3 * cout)
        result = None
        for b in range(3):
            start = STRIP + DILATION_STEP * (b - 1)
            term = total[:, start : start + width, b * cout : (b + 1) * cout]
            result = term if result is None else result + term
        out[...] = result.astype(jnp.bfloat16)


def call(kernel, operands, outs, scratch, flops):
    whole = pl.BlockSpec(memory_space=VMEM)
    size = sum(x.size * x.dtype.itemsize for x in operands) + sum(math.prod(o.shape) * o.dtype.itemsize for o in outs)
    return pl.pallas_call(
        kernel,
        out_shape=outs,
        in_specs=[pl.BlockSpec(memory_space=pltpu.SMEM)] + [whole] * (len(operands) - 1),
        out_specs=[whole] * len(outs),
        scratch_shapes=scratch,
        compiler_params=pltpu.CompilerParams(vmem_limit_bytes=48 * 1024 * 1024),
        cost_estimate=pl.CostEstimate(flops=flops, bytes_accessed=size if flops else 0, transcendentals=0),
    )(*operands)


def edges(blocks):
    width = blocks[0].shape[1]
    tails = jnp.stack([x[:, width - STRIP :] for x in blocks])
    heads = jnp.stack([x[:, :STRIP] for x in blocks])
    return tails, heads


def exchanged(tails, heads, count):
    left = lax.ppermute(tails, COLS, [(i, i + 1) for i in range(count - 1)])
    right = lax.ppermute(heads, COLS, [(i + 1, i) for i in range(count - 1)])
    return left, right


def joined(odd, own, other):
    low = jnp.where(odd == 1, other, own)
    high = jnp.where(odd == 1, own, other)
    return jnp.concatenate([low, high], axis=0)


def body(features, weight, cotangent):
    height, width, cin = features.shape
    cout = weight.shape[3]
    half = height // 2
    rows = lax.axis_size("rows")
    cols = lax.axis_size("x") * lax.axis_size("core")
    chips = rows * lax.axis_size("x")
    odd = lax.axis_index("rows") % 2
    core = lax.axis_index("core")
    par = jnp.stack([odd, core]).astype(jnp.int32)

    swap = [(i, i ^ 1) for i in range(rows)]
    other_core = [(0, 1), (1, 0)]
    up = [(i, i + 2 if i % 2 else i - 2) for i in range(rows)]
    near = [(i, j) for i, j in up if 0 <= j < rows]
    far = [(j, i) for i, j in near]
    fence = lax.optimization_barrier

    def pick(cells, which):
        return lax.dynamic_slice_in_dim(cells, which * half, half, 0)

    wide = width + 2 * STRIP
    share = 9 * cin // 2
    chunk = share // chips
    deep = -(-(chunk + 1) // STRIP) * STRIP
    flops = 2 * 9 * height * width * cin * cout

    d_own, d_give = (pick(cotangent, odd), pick(cotangent, 1 - odd))
    f_own, f_give = (pick(features, odd), pick(features, 1 - odd))
    d_par = lax.ppermute(d_give, "rows", swap)
    d_near = lax.ppermute(d_own, "rows", near)
    f_give, d_par = fence((f_give, d_par))
    f_par = lax.ppermute(f_give, "rows", swap)
    d_far = lax.ppermute(d_par, "rows", far)
    f_first, d_near = fence((f_own, d_near))
    f_near = lax.ppermute(f_first, "rows", near)
    f_far = lax.ppermute(f_par, "rows", far)
    d_blocks = (d_own, d_par, d_near, d_far)
    f_blocks = (f_own, f_par, f_near, f_far)
    d_left, d_right = exchanged(*edges(d_blocks), cols)

    part = jax.ShapeDtypeStruct((share, cout), jnp.float32)
    d_maps = [VMEM((4, half, wide, cout), jnp.bfloat16), VMEM((4, half, width, 3 * cout), jnp.bfloat16)]
    keep, give = call(
        kernel_grad,
        (par, f_own, f_par) + d_blocks + (d_left, d_right),
        [part, part],
        d_maps + [VMEM((9 * cin, cout), jnp.float32)],
        30 * flops,
    )
    given = lax.ppermute(give, "core", other_core)
    f_first, f_near = fence((f_own, f_near))
    f_tails, f_heads = edges((f_first, f_par, f_near, f_far))
    given, f_tails, f_heads = fence((given, f_tails, f_heads))

    (scaled,) = call(
        functools.partial(kernel_scale, chunk),
        (par, keep, given),
        [jax.ShapeDtypeStruct((chips, deep, cout), jnp.float32)],
        [],
        0,
    )
    scaled, f_tails, f_heads = fence((scaled.astype(jnp.float16), f_tails, f_heads))
    f_blocks = (f_own, f_par, f_near, f_far)
    got = lax.all_to_all(scaled, CHIPS, 0, 0)

    d_left, _ = fence((d_left, scaled))
    half_grad = jax.ShapeDtypeStruct((half, width, cin), jnp.bfloat16)
    g_own, g_par = call(
        kernel_back, (par, weight) + d_blocks + (d_left, d_right), [half_grad, half_grad], d_maps, 0
    )
    g_other = lax.ppermute(g_par, "rows", swap)

    f_left, f_right = exchanged(f_tails, f_heads, cols)

    half_out = jax.ShapeDtypeStruct((half, width, cout), jnp.bfloat16)
    o_own, o_par = call(
        kernel_out,
        (par, weight) + f_blocks + (f_left, f_right),
        [half_out, half_out],
        [VMEM((4, half, wide, cin), jnp.bfloat16)],
        0,
    )
    got, o_par = fence((got, o_par))
    o_other = lax.ppermute(o_par, "rows", swap)

    levels = got[:, chunk : chunk + 1].astype(jnp.float32)
    highest = jnp.max(levels, axis=0, keepdims=True)
    shares = got.astype(jnp.float32) * jnp.exp2(levels - highest)
    mine = jnp.sum(shares, axis=0, keepdims=True) * (1.0 / chips)
    place = lax.broadcasted_iota(jnp.int32, mine.shape, 1)
    mine = jnp.where(place < chunk, mine, highest).astype(jnp.float16)
    mine, g_other = fence((mine, g_other))
    spread = lax.all_to_all(jnp.broadcast_to(mine, (chips, deep, cout)), CHIPS, 0, 0)
    other = lax.ppermute(spread, "core", other_core)

    norm = chips / jnp.sqrt(jnp.float32(height * width * chips * 2))

    def restored(low, high):
        picked = jnp.where(core == 0, low, high)
        factor = jnp.exp2(picked[:1, chunk : chunk + 1].astype(jnp.float32) - TOP) * norm
        return (picked[:, :chunk].astype(jnp.float32) * factor).reshape(share, cout)

    weight_grad = jnp.concatenate([restored(spread, other), restored(other, spread)], axis=0)
    return (
        joined(odd, o_own, o_other),
        joined(odd, g_own, g_other),
        weight_grad.reshape(weight.shape),
    )


def solution(mesh):
    rows, cols = (mesh.shape["rows"], mesh.shape["cols"])
    fine = Mesh(mesh.devices.reshape(rows, cols // 2, 2), ("rows",) + COLS)
    placed = P("rows", COLS, None)
    return jax.shard_map(
        body,
        mesh=fine,
        in_specs=(placed, P(), placed),
        out_specs=(placed, placed, P()),
        check_vma=False,
    )
```

```python
import functools
import math

import jax
import jax.numpy as jnp
from jax import lax
from jax.experimental import pallas as pl
from jax.experimental.pallas import tpu as pltpu
from jax.sharding import Mesh
from jax.sharding import PartitionSpec as P

DILATION_STEP = 12
STRIP = 16
TOP = 14
COLS = ("x", "core")
CHIPS = ("rows", "x")
VMEM = pltpu.VMEM


def slots(odd):
    return (1 + odd, 2 - odd, 3 * (1 - odd), 3 * odd)


def gather_map(odd, blocks, left, right, ext):
    width = blocks[0].shape[1]
    depth = ext.shape[3]
    for place, (block, slot) in enumerate(zip(blocks, slots(odd))):
        first = 0 if depth > block.shape[2] // 2 else block.shape[2] - depth
        ext[slot, :, pl.ds(STRIP, width), :] = block[:, :, first : first + depth]
        ext[slot, :, pl.ds(0, STRIP), :] = left[place]
        ext[slot, :, pl.ds(STRIP + width, STRIP), :] = right[place]


def shift_columns(ext, shifted, width):
    cout = ext.shape[3]
    for slot in range(4):
        whole = ext[slot].astype(jnp.float32)
        for q in range(3):
            start = STRIP + DILATION_STEP * (q - 1)
            shifted[slot, :, :, pl.ds(q * cout, cout)] = whole[:, start : start + width].astype(jnp.bfloat16)


def kernel_grad(par, f_own, f_par, d_own, d_par, d_near, d_far, left, right, keep, give, ext, shifted, acc):
    odd, core = (par[0], par[1])
    half, width, cout = d_own.shape
    cin = f_own.shape[2]
    pixels = half * width
    gather_map(odd, (d_own, d_par, d_near, d_far), left, right, ext)
    shift_columns(ext, shifted, width)
    own, partner = slots(odd)[:2]
    total = None
    for block, slot in ((f_own, own), (f_par, partner)):
        lhs = block[...].reshape(pixels, cin)
        rhs = jnp.concatenate([shifted[slot + 1 - a].reshape(pixels, 3 * cout) for a in range(3)], axis=1)
        term = lax.dot_general(lhs, rhs, (((0,), (0,)), ((), ())), preferred_element_type=jnp.float32)
        total = term if total is None else total + term
    for a in range(3):
        for b in range(3):
            start = (3 * a + 2 - b) * cout
            acc[pl.ds((3 * a + b) * cin, cin), :] = total[:, start : start + cout]
    size = keep.shape[0]
    keep[...] = acc[pl.ds(core * size, size), :]
    give[...] = acc[pl.ds((1 - core) * size, size), :]


def kernel_scale(chunk, par, keep, given, out):
    total = keep[...] + given[...]
    size, cout = keep.shape
    top = jnp.max(jnp.abs(total).reshape(size // 8, 8, cout), axis=0)
    most = jnp.max(jnp.max(top, axis=0, keepdims=True), axis=1, keepdims=True)
    level = jnp.ceil(jnp.log2(jnp.maximum(jnp.broadcast_to(most, (8, cout)), 2.0**-110)))
    scaled = total * jnp.exp2(TOP - level)[:1]
    for c in range(out.shape[0]):
        out[c, pl.ds(0, chunk), :] = scaled[c * chunk : (c + 1) * chunk]
        out[c, pl.ds(chunk, out.shape[1] - chunk), :] = jnp.broadcast_to(level[:1], (out.shape[1] - chunk, cout))


def kernel_back(par, w, d_own, d_par, d_near, d_far, left, right, out_own, out_par, ext, shifted):
    odd = par[0]
    half, width, cout = d_own.shape
    cin = w.shape[2]
    pixels = half * width
    gather_map(odd, (d_own, d_par, d_near, d_far), left, right, ext)
    shift_columns(ext, shifted, width)
    own, partner = slots(odd)[:2]
    for out, slot in ((out_own, own), (out_par, partner)):
        total = None
        for a in range(3):
            lhs = shifted[slot + 1 - a].reshape(pixels, 3 * cout)
            rhs = jnp.concatenate([w[a, 2 - q] for q in range(3)], axis=1)
            term = lax.dot_general(lhs, rhs, (((1,), (1,)), ((), ())), preferred_element_type=jnp.float32)
            total = term if total is None else total + term
        out[...] = total.astype(jnp.bfloat16).reshape(half, width, cin)


def kernel_out(par, w, f_own, f_par, f_near, f_far, left, right, out_own, out_par, ext):
    odd = par[0]
    half, width, cout = out_own.shape
    cin = f_own.shape[2]
    wide = width + 2 * STRIP
    gather_map(odd, (f_own, f_par, f_near, f_far), left, right, ext)
    own, partner = slots(odd)[:2]
    for out, slot in ((out_own, own), (out_par, partner)):
        total = None
        for a in range(3):
            lhs = ext[slot + a - 1].reshape(half * wide, cin)
            rhs = jnp.concatenate([w[a, b] for b in range(3)], axis=1)
            term = jnp.dot(lhs, rhs, preferred_element_type=jnp.float32)
            total = term if total is None else total + term
        total = total.reshape(half, wide, 3 * cout)
        result = None
        for b in range(3):
            start = STRIP + DILATION_STEP * (b - 1)
            term = total[:, start : start + width, b * cout : (b + 1) * cout]
            result = term if result is None else result + term
        out[...] = result.astype(jnp.bfloat16)


def call(kernel, operands, outs, scratch, flops):
    whole = pl.BlockSpec(memory_space=VMEM)
    size = sum(x.size * x.dtype.itemsize for x in operands) + sum(math.prod(o.shape) * o.dtype.itemsize for o in outs)
    return pl.pallas_call(
        kernel,
        out_shape=outs,
        in_specs=[pl.BlockSpec(memory_space=pltpu.SMEM)] + [whole] * (len(operands) - 1),
        out_specs=[whole] * len(outs),
        scratch_shapes=scratch,
        compiler_params=pltpu.CompilerParams(vmem_limit_bytes=20 * 1024 * 1024),
        cost_estimate=pl.CostEstimate(flops=flops, bytes_accessed=size if flops else 0, transcendentals=0),
    )(*operands)


def edges(blocks, first, depth):
    width = blocks[0].shape[1]
    parts = [x if x.shape[2] == depth else x[:, :, first : first + depth] for x in blocks]
    tails = jnp.stack([x[:, width - STRIP :] for x in parts])
    heads = jnp.stack([x[:, :STRIP] for x in parts])
    return tails, heads


def exchanged(tails, heads, count):
    left = lax.ppermute(tails, COLS, [(i, i + 1) for i in range(count - 1)])
    right = lax.ppermute(heads, COLS, [(i + 1, i) for i in range(count - 1)])
    return left, right


def joined(odd, own, other):
    low = jnp.where(odd == 1, other, own)
    high = jnp.where(odd == 1, own, other)
    return jnp.concatenate([low, high], axis=0)


def body(features, weight, cotangent):
    height, width, cin = features.shape
    cout = weight.shape[3]
    half = height // 2
    rows = lax.axis_size("rows")
    cols = lax.axis_size("x") * lax.axis_size("core")
    chips = rows * lax.axis_size("x")
    odd = lax.axis_index("rows") % 2
    core = lax.axis_index("core")
    par = jnp.stack([odd, core]).astype(jnp.int32)

    swap = [(i, i ^ 1) for i in range(rows)]
    other_core = [(0, 1), (1, 0)]
    up = [(i, i + 2 if i % 2 else i - 2) for i in range(rows)]
    near = [(i, j) for i, j in up if 0 <= j < rows]
    far = [(j, i) for i, j in near]
    fence = lax.optimization_barrier

    def pick(cells, which):
        return lax.dynamic_slice_in_dim(cells, which * half, half, 0)

    wide = width + 2 * STRIP
    share = 9 * cin // 2
    chunk = share // chips
    deep = -(-(chunk + 1) // STRIP) * STRIP
    flops = 2 * 9 * height * width * cin * cout

    d_own, d_give = (pick(cotangent, odd), pick(cotangent, 1 - odd))
    f_own, f_give = (pick(features, odd), pick(features, 1 - odd))
    both = lax.ppermute(jnp.concatenate([f_own, d_own], axis=2), "rows", near)
    d_par = lax.ppermute(d_give, "rows", swap)
    f_give, d_par = fence((f_give, d_par))
    f_par = lax.ppermute(f_give, "rows", swap)
    d_far = lax.ppermute(d_par, "rows", far)
    f_far = lax.ppermute(f_par, "rows", far)
    d_blocks = (d_own, d_par, both, d_far)
    f_blocks = (f_own, f_par, both, f_far)
    d_left, d_right = exchanged(*edges(d_blocks, cin, cout), cols)

    part = jax.ShapeDtypeStruct((share, cout), jnp.float32)
    d_maps = [VMEM((4, half, wide, cout), jnp.bfloat16), VMEM((4, half, width, 3 * cout), jnp.bfloat16)]
    keep, give = call(
        kernel_grad,
        (par, f_own, f_par) + d_blocks + (d_left, d_right),
        [part, part],
        d_maps + [VMEM((9 * cin, cout), jnp.float32)],
        30 * flops,
    )
    given = lax.ppermute(give, "core", other_core)
    f_tails, f_heads = edges(f_blocks, 0, cin)
    half_grad = jax.ShapeDtypeStruct((half, width, cin), jnp.bfloat16)
    g_own, g_par = call(
        kernel_back, (par, weight) + d_blocks + (d_left, d_right), [half_grad, half_grad], d_maps, 0
    )
    g_other = lax.ppermute(g_par, "rows", swap)
    given, f_tails, f_heads, g_par = fence((given, f_tails, f_heads, g_par))

    (scaled,) = call(
        functools.partial(kernel_scale, chunk),
        (par, keep, given),
        [jax.ShapeDtypeStruct((chips, deep, cout), jnp.float32)],
        [],
        0,
    )
    scaled, f_tails, f_heads = fence((scaled.astype(jnp.float16), f_tails, f_heads))
    got = lax.all_to_all(scaled, CHIPS, 0, 0)

    f_left, f_right = exchanged(f_tails, f_heads, cols)
    f_left, g_other = fence((f_left, g_other))

    half_out = jax.ShapeDtypeStruct((half, width, cout), jnp.bfloat16)
    o_own, o_par = call(
        kernel_out,
        (par, weight) + f_blocks + (f_left, f_right),
        [half_out, half_out],
        [VMEM((4, half, wide, cin), jnp.bfloat16)],
        0,
    )
    got, o_par = fence((got, o_par))
    o_other = lax.ppermute(o_par, "rows", swap)

    levels = got[:, chunk : chunk + 1].astype(jnp.float32)
    highest = jnp.max(levels, axis=0, keepdims=True)
    shares = got.astype(jnp.float32) * jnp.exp2(levels - highest)
    mine = jnp.sum(shares, axis=0, keepdims=True) * (1.0 / chips)
    place = lax.broadcasted_iota(jnp.int32, mine.shape, 1)
    mine = jnp.where(place < chunk, mine, highest).astype(jnp.float16)
    spread = lax.all_to_all(jnp.broadcast_to(mine, (chips, deep, cout)), CHIPS, 0, 0)
    other = lax.ppermute(spread, "core", other_core)

    norm = chips / jnp.sqrt(jnp.float32(height * width * chips * 2))

    def restored(low, high):
        picked = jnp.where(core == 0, low, high)
        factor = jnp.exp2(picked[:1, chunk : chunk + 1].astype(jnp.float32) - TOP) * norm
        return (picked[:, :chunk].astype(jnp.float32) * factor).reshape(share, cout)

    weight_grad = jnp.concatenate([restored(spread, other), restored(other, spread)], axis=0)
    return (
        joined(odd, o_own, o_other),
        joined(odd, g_own, g_other),
        weight_grad.reshape(weight.shape),
    )


def solution(mesh):
    rows, cols = (mesh.shape["rows"], mesh.shape["cols"])
    fine = Mesh(mesh.devices.reshape(rows, cols // 2, 2), ("rows",) + COLS)
    placed = P("rows", COLS, None)
    return jax.shard_map(
        body,
        mesh=fine,
        in_specs=(placed, P(), placed),
        out_specs=(placed, placed, P()),
        check_vma=False,
    )
```

```python
import functools
import math

import jax
import jax.numpy as jnp
from jax import lax
from jax.experimental import pallas as pl
from jax.experimental.pallas import tpu as pltpu
from jax.sharding import Mesh
from jax.sharding import PartitionSpec as P

DILATION_STEP = 12
STRIP = 16
TOP = 14
COLS = ("x", "core")
CHIPS = ("rows", "x")
VMEM = pltpu.VMEM


def slots(odd):
    return (1 + odd, 2 - odd, 3 * (1 - odd), 3 * odd)


def gather_map(odd, blocks, left, right, ext):
    width = blocks[0].shape[1]
    for place, (block, slot) in enumerate(zip(blocks, slots(odd))):
        ext[slot, :, pl.ds(STRIP, width), :] = block[...]
        ext[slot, :, pl.ds(0, STRIP), :] = left[place]
        ext[slot, :, pl.ds(STRIP + width, STRIP), :] = right[place]


def shift_columns(ext, shifted, width):
    cout = ext.shape[3]
    for slot in range(4):
        whole = ext[slot].astype(jnp.float32)
        for q in range(3):
            start = STRIP + DILATION_STEP * (q - 1)
            shifted[slot, :, :, pl.ds(q * cout, cout)] = whole[:, start : start + width].astype(jnp.bfloat16)


def kernel_grad(par, f_own, f_par, d_own, d_par, d_near, d_far, left, right, keep, give, ext, shifted, acc):
    odd, core = (par[0], par[1])
    half, width, cout = d_own.shape
    cin = f_own.shape[2]
    pixels = half * width
    gather_map(odd, (d_own, d_par, d_near, d_far), left, right, ext)
    shift_columns(ext, shifted, width)
    own, partner = slots(odd)[:2]
    total = None
    for block, slot in ((f_own, own), (f_par, partner)):
        lhs = block[...].reshape(pixels, cin)
        rhs = jnp.concatenate([shifted[slot + 1 - a].reshape(pixels, 3 * cout) for a in range(3)], axis=1)
        term = lax.dot_general(lhs, rhs, (((0,), (0,)), ((), ())), preferred_element_type=jnp.float32)
        total = term if total is None else total + term
    for a in range(3):
        for b in range(3):
            start = (3 * a + 2 - b) * cout
            acc[pl.ds((3 * a + b) * cin, cin), :] = total[:, start : start + cout]
    size = keep.shape[0]
    keep[...] = acc[pl.ds(core * size, size), :]
    give[...] = acc[pl.ds((1 - core) * size, size), :]


def kernel_scale(chunk, par, keep, given, out):
    total = keep[...] + given[...]
    size, cout = keep.shape
    top = jnp.max(jnp.abs(total).reshape(size // 8, 8, cout), axis=0)
    most = jnp.max(jnp.max(top, axis=0, keepdims=True), axis=1, keepdims=True)
    level = jnp.ceil(jnp.log2(jnp.maximum(jnp.broadcast_to(most, (8, cout)), 2.0**-110)))
    scaled = total * jnp.exp2(TOP - level)[:1]
    for c in range(out.shape[0]):
        out[c, pl.ds(0, chunk), :] = scaled[c * chunk : (c + 1) * chunk]
        out[c, pl.ds(chunk, out.shape[1] - chunk), :] = jnp.broadcast_to(level[:1], (out.shape[1] - chunk, cout))


def kernel_back(par, w, d_own, d_par, d_near, d_far, left, right, out_own, out_par, ext, shifted):
    odd = par[0]
    half, width, cout = d_own.shape
    cin = w.shape[2]
    pixels = half * width
    gather_map(odd, (d_own, d_par, d_near, d_far), left, right, ext)
    shift_columns(ext, shifted, width)
    own, partner = slots(odd)[:2]
    for out, slot in ((out_own, own), (out_par, partner)):
        total = None
        for a in range(3):
            lhs = shifted[slot + 1 - a].reshape(pixels, 3 * cout)
            rhs = jnp.concatenate([w[a, 2 - q] for q in range(3)], axis=1)
            term = lax.dot_general(lhs, rhs, (((1,), (1,)), ((), ())), preferred_element_type=jnp.float32)
            total = term if total is None else total + term
        out[...] = total.astype(jnp.bfloat16).reshape(half, width, cin)


def kernel_out(par, w, f_own, f_par, f_near, f_far, left, right, out_own, out_par, ext):
    odd = par[0]
    half, width, cout = out_own.shape
    cin = f_own.shape[2]
    wide = width + 2 * STRIP
    gather_map(odd, (f_own, f_par, f_near, f_far), left, right, ext)
    own, partner = slots(odd)[:2]
    for out, slot in ((out_own, own), (out_par, partner)):
        total = None
        for a in range(3):
            lhs = ext[slot + a - 1].reshape(half * wide, cin)
            rhs = jnp.concatenate([w[a, b] for b in range(3)], axis=1)
            term = jnp.dot(lhs, rhs, preferred_element_type=jnp.float32)
            total = term if total is None else total + term
        total = total.reshape(half, wide, 3 * cout)
        result = None
        for b in range(3):
            start = STRIP + DILATION_STEP * (b - 1)
            term = total[:, start : start + width, b * cout : (b + 1) * cout]
            result = term if result is None else result + term
        out[...] = result.astype(jnp.bfloat16)


def call(kernel, operands, outs, scratch, flops):
    whole = pl.BlockSpec(memory_space=VMEM)
    size = sum(x.size * x.dtype.itemsize for x in operands) + sum(math.prod(o.shape) * o.dtype.itemsize for o in outs)
    return pl.pallas_call(
        kernel,
        out_shape=outs,
        in_specs=[pl.BlockSpec(memory_space=pltpu.SMEM)] + [whole] * (len(operands) - 1),
        out_specs=[whole] * len(outs),
        scratch_shapes=scratch,
        compiler_params=pltpu.CompilerParams(vmem_limit_bytes=12 * 1024 * 1024),
        cost_estimate=pl.CostEstimate(flops=flops, bytes_accessed=size if flops else 0, transcendentals=0),
    )(*operands)


def edges(blocks):
    width = blocks[0].shape[1]
    tails = jnp.stack([x[:, width - STRIP :] for x in blocks])
    heads = jnp.stack([x[:, :STRIP] for x in blocks])
    return tails, heads


def exchanged(tails, heads, count):
    left = lax.ppermute(tails, COLS, [(i, i + 1) for i in range(count - 1)])
    right = lax.ppermute(heads, COLS, [(i + 1, i) for i in range(count - 1)])
    return left, right


def joined(odd, own, other):
    low = jnp.where(odd == 1, other, own)
    high = jnp.where(odd == 1, own, other)
    return jnp.concatenate([low, high], axis=0)


def body(features, weight, cotangent):
    height, width, cin = features.shape
    cout = weight.shape[3]
    half = height // 2
    rows = lax.axis_size("rows")
    cols = lax.axis_size("x") * lax.axis_size("core")
    chips = rows * lax.axis_size("x")
    odd = lax.axis_index("rows") % 2
    core = lax.axis_index("core")
    par = jnp.stack([odd, core]).astype(jnp.int32)

    swap = [(i, i ^ 1) for i in range(rows)]
    other_core = [(0, 1), (1, 0)]
    up = [(i, i + 2 if i % 2 else i - 2) for i in range(rows)]
    near = [(i, j) for i, j in up if 0 <= j < rows]
    far = [(j, i) for i, j in near]
    fence = lax.optimization_barrier

    def pick(cells, which):
        return lax.dynamic_slice_in_dim(cells, which * half, half, 0)

    wide = width + 2 * STRIP
    share = 9 * cin // 2
    chunk = share // chips
    deep = -(-(chunk + 1) // STRIP) * STRIP
    flops = 2 * 9 * height * width * cin * cout

    d_own, d_give = (pick(cotangent, odd), pick(cotangent, 1 - odd))
    f_own, f_give = (pick(features, odd), pick(features, 1 - odd))
    d_par = lax.ppermute(d_give, "rows", swap)
    d_near = lax.ppermute(d_own, "rows", near)
    f_give, d_par = fence((f_give, d_par))
    f_par = lax.ppermute(f_give, "rows", swap)
    d_far = lax.ppermute(d_par, "rows", far)
    f_first, d_far = fence((f_own, d_far))
    f_near = lax.ppermute(f_first, "rows", near)
    f_far = lax.ppermute(f_par, "rows", far)
    d_blocks = (d_own, d_par, d_near, d_far)
    f_blocks = (f_own, f_par, f_near, f_far)
    d_left, d_right = exchanged(*edges(d_blocks), cols)

    part = jax.ShapeDtypeStruct((share, cout), jnp.float32)
    d_maps = [VMEM((4, half, wide, cout), jnp.bfloat16), VMEM((4, half, width, 3 * cout), jnp.bfloat16)]
    keep, give = call(
        kernel_grad,
        (par, f_own, f_par) + d_blocks + (d_left, d_right),
        [part, part],
        d_maps + [VMEM((9 * cin, cout), jnp.float32)],
        30 * flops,
    )
    given = lax.ppermute(give, "core", other_core)
    f_tails, f_heads = edges(f_blocks)
    half_grad = jax.ShapeDtypeStruct((half, width, cin), jnp.bfloat16)
    g_own, g_par = call(
        kernel_back, (par, weight) + d_blocks + (d_left, d_right), [half_grad, half_grad], d_maps, 0
    )
    g_other = lax.ppermute(g_par, "rows", swap)
    given, f_tails, f_heads, g_par = fence((given, f_tails, f_heads, g_par))

    (scaled,) = call(
        functools.partial(kernel_scale, chunk),
        (par, keep, given),
        [jax.ShapeDtypeStruct((chips, deep, cout), jnp.float32)],
        [],
        0,
    )
    scaled, f_tails, f_heads = fence((scaled.astype(jnp.float16), f_tails, f_heads))
    got = lax.all_to_all(scaled, CHIPS, 0, 0)
    g_own, _ = fence((g_own, scaled))

    f_left, f_right = exchanged(f_tails, f_heads, cols)

    half_out = jax.ShapeDtypeStruct((half, width, cout), jnp.bfloat16)
    o_own, o_par = call(
        kernel_out,
        (par, weight) + f_blocks + (f_left, f_right),
        [half_out, half_out],
        [VMEM((4, half, wide, cin), jnp.bfloat16)],
        0,
    )
    got, o_par = fence((got, o_par))
    o_other = lax.ppermute(o_par, "rows", swap)

    levels = got[:, chunk : chunk + 1].astype(jnp.float32)
    highest = jnp.max(levels, axis=0, keepdims=True)
    shares = got.astype(jnp.float32) * jnp.exp2(levels - highest)
    mine = jnp.sum(shares, axis=0, keepdims=True) * (1.0 / chips)
    place = lax.broadcasted_iota(jnp.int32, mine.shape, 1)
    mine = jnp.where(place < chunk, mine, highest).astype(jnp.float16)
    spread = lax.all_to_all(jnp.broadcast_to(mine, (chips, deep, cout)), CHIPS, 0, 0)
    other = lax.ppermute(spread, "core", other_core)

    norm = chips / jnp.sqrt(jnp.float32(height * width * chips * 2))

    def restored(low, high):
        picked = jnp.where(core == 0, low, high)
        factor = jnp.exp2(picked[:1, chunk : chunk + 1].astype(jnp.float32) - TOP) * norm
        return (picked[:, :chunk].astype(jnp.float32) * factor).reshape(share, cout)

    weight_grad = jnp.concatenate([restored(spread, other), restored(other, spread)], axis=0)
    return (
        joined(odd, o_own, o_other),
        joined(odd, g_own, g_other),
        weight_grad.reshape(weight.shape),
    )


def solution(mesh):
    rows, cols = (mesh.shape["rows"], mesh.shape["cols"])
    fine = Mesh(mesh.devices.reshape(rows, cols // 2, 2), ("rows",) + COLS)
    placed = P("rows", COLS, None)
    return jax.shard_map(
        body,
        mesh=fine,
        in_specs=(placed, P(), placed),
        out_specs=(placed, placed, P()),
        check_vma=False,
    )
```

```python
import functools
import math

import jax
import jax.numpy as jnp
from jax import lax
from jax.experimental import pallas as pl
from jax.experimental.pallas import tpu as pltpu
from jax.sharding import Mesh
from jax.sharding import PartitionSpec as P

DILATION_STEP = 12
STRIP = 16
TOP = 14
COLS = ("x", "core")
CHIPS = ("rows", "x")
VMEM = pltpu.VMEM


def slots(odd):
    return (1 + odd, 2 - odd, 3 * (1 - odd), 3 * odd)


def gather_map(odd, blocks, left, right, ext):
    width = blocks[0].shape[1]
    for place, (block, slot) in enumerate(zip(blocks, slots(odd))):
        ext[slot, :, pl.ds(STRIP, width), :] = block[...]
        ext[slot, :, pl.ds(0, STRIP), :] = left[place]
        ext[slot, :, pl.ds(STRIP + width, STRIP), :] = right[place]


def shift_columns(ext, shifted, width):
    cout = ext.shape[3]
    for slot in range(4):
        whole = ext[slot].astype(jnp.float32)
        for q in range(3):
            start = STRIP + DILATION_STEP * (q - 1)
            shifted[slot, :, :, pl.ds(q * cout, cout)] = whole[:, start : start + width].astype(jnp.bfloat16)


def kernel_grad(par, f_own, f_par, d_own, d_par, d_near, d_far, left, right, keep, give, ext, shifted, acc):
    odd, core = (par[0], par[1])
    half, width, cout = d_own.shape
    cin = f_own.shape[2]
    pixels = half * width
    gather_map(odd, (d_own, d_par, d_near, d_far), left, right, ext)
    shift_columns(ext, shifted, width)
    own, partner = slots(odd)[:2]
    total = None
    for block, slot in ((f_own, own), (f_par, partner)):
        lhs = block[...].reshape(pixels, cin)
        rhs = jnp.concatenate([shifted[slot + 1 - a].reshape(pixels, 3 * cout) for a in range(3)], axis=1)
        term = lax.dot_general(lhs, rhs, (((0,), (0,)), ((), ())), preferred_element_type=jnp.float32)
        total = term if total is None else total + term
    for a in range(3):
        for b in range(3):
            start = (3 * a + 2 - b) * cout
            acc[pl.ds((3 * a + b) * cin, cin), :] = total[:, start : start + cout]
    size = keep.shape[0]
    keep[...] = acc[pl.ds(core * size, size), :]
    give[...] = acc[pl.ds((1 - core) * size, size), :]


def kernel_scale(chunk, par, keep, given, out):
    total = keep[...] + given[...]
    size, cout = keep.shape
    top = jnp.max(jnp.abs(total).reshape(size // 8, 8, cout), axis=0)
    most = jnp.max(jnp.max(top, axis=0, keepdims=True), axis=1, keepdims=True)
    level = jnp.ceil(jnp.log2(jnp.maximum(jnp.broadcast_to(most, (8, cout)), 2.0**-110)))
    scaled = total * jnp.exp2(TOP - level)[:1]
    for c in range(out.shape[0]):
        out[c, pl.ds(0, chunk), :] = scaled[c * chunk : (c + 1) * chunk]
        out[c, pl.ds(chunk, out.shape[1] - chunk), :] = jnp.broadcast_to(level[:1], (out.shape[1] - chunk, cout))


def kernel_sum(chunk, par, got, out):
    chips, deep, cout = got.shape
    levels = [got[i, pl.ds(chunk, 1), :] for i in range(chips)]
    highest = functools.reduce(jnp.maximum, levels)
    total = None
    for i in range(chips):
        term = got[i, pl.ds(0, chunk), :] * jnp.exp2(levels[i] - highest)
        total = term if total is None else total + term
    out[pl.ds(0, chunk), :] = total * (1.0 / chips)
    out[pl.ds(chunk, deep - chunk), :] = jnp.broadcast_to(highest, (deep - chunk, cout))


def kernel_back(par, w, d_own, d_par, d_near, d_far, left, right, out_own, out_par, ext, shifted):
    odd = par[0]
    half, width, cout = d_own.shape
    cin = w.shape[2]
    pixels = half * width
    gather_map(odd, (d_own, d_par, d_near, d_far), left, right, ext)
    shift_columns(ext, shifted, width)
    own, partner = slots(odd)[:2]
    for out, slot in ((out_own, own), (out_par, partner)):
        total = None
        for a in range(3):
            lhs = shifted[slot + 1 - a].reshape(pixels, 3 * cout)
            rhs = jnp.concatenate([w[a, 2 - q] for q in range(3)], axis=1)
            term = lax.dot_general(lhs, rhs, (((1,), (1,)), ((), ())), preferred_element_type=jnp.float32)
            total = term if total is None else total + term
        out[...] = total.astype(jnp.bfloat16).reshape(half, width, cin)


def kernel_out(par, w, f_own, f_par, f_near, f_far, left, right, out_own, out_par, ext):
    odd = par[0]
    half, width, cout = out_own.shape
    cin = f_own.shape[2]
    wide = width + 2 * STRIP
    gather_map(odd, (f_own, f_par, f_near, f_far), left, right, ext)
    own, partner = slots(odd)[:2]
    for out, slot in ((out_own, own), (out_par, partner)):
        total = None
        for a in range(3):
            lhs = ext[slot + a - 1].reshape(half * wide, cin)
            rhs = jnp.concatenate([w[a, b] for b in range(3)], axis=1)
            term = jnp.dot(lhs, rhs, preferred_element_type=jnp.float32)
            total = term if total is None else total + term
        total = total.reshape(half, wide, 3 * cout)
        result = None
        for b in range(3):
            start = STRIP + DILATION_STEP * (b - 1)
            term = total[:, start : start + width, b * cout : (b + 1) * cout]
            result = term if result is None else result + term
        out[...] = result.astype(jnp.bfloat16)


def call(kernel, operands, outs, scratch, flops):
    whole = pl.BlockSpec(memory_space=VMEM)
    size = sum(x.size * x.dtype.itemsize for x in operands) + sum(math.prod(o.shape) * o.dtype.itemsize for o in outs)
    return pl.pallas_call(
        kernel,
        out_shape=outs,
        in_specs=[pl.BlockSpec(memory_space=pltpu.SMEM)] + [whole] * (len(operands) - 1),
        out_specs=[whole] * len(outs),
        scratch_shapes=scratch,
        compiler_params=pltpu.CompilerParams(vmem_limit_bytes=12 * 1024 * 1024),
        cost_estimate=pl.CostEstimate(flops=flops, bytes_accessed=size if flops else 0, transcendentals=0),
    )(*operands)


def edges(blocks):
    width = blocks[0].shape[1]
    tails = jnp.stack([x[:, width - STRIP :] for x in blocks])
    heads = jnp.stack([x[:, :STRIP] for x in blocks])
    return tails, heads


def exchanged(tails, heads, count):
    left = lax.ppermute(tails, COLS, [(i, i + 1) for i in range(count - 1)])
    right = lax.ppermute(heads, COLS, [(i + 1, i) for i in range(count - 1)])
    return left, right


def joined(odd, own, other):
    low = jnp.where(odd == 1, other, own)
    high = jnp.where(odd == 1, own, other)
    return jnp.concatenate([low, high], axis=0)


def body(features, weight, cotangent):
    height, width, cin = features.shape
    cout = weight.shape[3]
    half = height // 2
    rows = lax.axis_size("rows")
    cols = lax.axis_size("x") * lax.axis_size("core")
    chips = rows * lax.axis_size("x")
    odd = lax.axis_index("rows") % 2
    core = lax.axis_index("core")
    par = jnp.stack([odd, core]).astype(jnp.int32)

    swap = [(i, i ^ 1) for i in range(rows)]
    other_core = [(0, 1), (1, 0)]
    up = [(i, i + 2 if i % 2 else i - 2) for i in range(rows)]
    near = [(i, j) for i, j in up if 0 <= j < rows]
    far = [(j, i) for i, j in near]
    fence = lax.optimization_barrier

    def pick(cells, which):
        return lax.dynamic_slice_in_dim(cells, which * half, half, 0)

    wide = width + 2 * STRIP
    share = 9 * cin // 2
    chunk = share // chips
    deep = -(-(chunk + 1) // STRIP) * STRIP
    flops = 2 * 9 * height * width * cin * cout

    d_own, d_give = (pick(cotangent, odd), pick(cotangent, 1 - odd))
    f_own, f_give = (pick(features, odd), pick(features, 1 - odd))
    d_par = lax.ppermute(d_give, "rows", swap)
    d_near = lax.ppermute(d_own, "rows", near)
    f_give, d_par = fence((f_give, d_par))
    f_par = lax.ppermute(f_give, "rows", swap)
    d_far = lax.ppermute(d_par, "rows", far)
    f_first, d_far = fence((f_own, d_far))
    f_near = lax.ppermute(f_first, "rows", near)
    f_far = lax.ppermute(f_par, "rows", far)
    d_blocks = (d_own, d_par, d_near, d_far)
    f_blocks = (f_own, f_par, f_near, f_far)
    d_left, d_right = exchanged(*edges(d_blocks), cols)

    part = jax.ShapeDtypeStruct((share, cout), jnp.float32)
    d_maps = [VMEM((4, half, wide, cout), jnp.bfloat16), VMEM((4, half, width, 3 * cout), jnp.bfloat16)]
    keep, give = call(
        kernel_grad,
        (par, f_own, f_par) + d_blocks + (d_left, d_right),
        [part, part],
        d_maps + [VMEM((9 * cin, cout), jnp.float32)],
        30 * flops,
    )
    given = lax.ppermute(give, "core", other_core)
    f_tails, f_heads = edges(f_blocks)
    given, f_tails, f_heads = fence((given, f_tails, f_heads))

    (scaled,) = call(
        functools.partial(kernel_scale, chunk),
        (par, keep, given),
        [jax.ShapeDtypeStruct((chips, deep, cout), jnp.float32)],
        [],
        0,
    )
    scaled, f_tails, f_heads = fence((scaled.astype(jnp.float16), f_tails, f_heads))
    got = lax.all_to_all(scaled, CHIPS, 0, 0)
    d_left, _ = fence((d_left, scaled))
    half_grad = jax.ShapeDtypeStruct((half, width, cin), jnp.bfloat16)
    g_own, g_par = call(
        kernel_back, (par, weight) + d_blocks + (d_left, d_right), [half_grad, half_grad], d_maps, 0
    )
    g_other = lax.ppermute(g_par, "rows", swap)
    got, g_par = fence((got, g_par))

    f_left, f_right = exchanged(f_tails, f_heads, cols)

    (mine,) = call(
        functools.partial(kernel_sum, chunk),
        (par, got.astype(jnp.float32)),
        [jax.ShapeDtypeStruct((deep, cout), jnp.float32)],
        [],
        0,
    )
    mine = mine.astype(jnp.float16)
    f_left, copies = fence((f_left, jnp.broadcast_to(mine[None], (chips, deep, cout))))
    spread = lax.all_to_all(copies, CHIPS, 0, 0)
    other = lax.ppermute(spread, "core", other_core)

    half_out = jax.ShapeDtypeStruct((half, width, cout), jnp.bfloat16)
    o_own, o_par = call(
        kernel_out,
        (par, weight) + f_blocks + (f_left, f_right),
        [half_out, half_out],
        [VMEM((4, half, wide, cin), jnp.bfloat16)],
        0,
    )
    o_other = lax.ppermute(o_par, "rows", swap)

    norm = chips / jnp.sqrt(jnp.float32(height * width * chips * 2))

    def restored(low, high):
        picked = jnp.where(core == 0, low, high)
        factor = jnp.exp2(picked[:1, chunk : chunk + 1].astype(jnp.float32) - TOP) * norm
        return (picked[:, :chunk].astype(jnp.float32) * factor).reshape(share, cout)

    weight_grad = jnp.concatenate([restored(spread, other), restored(other, spread)], axis=0)
    return (
        joined(odd, o_own, o_other),
        joined(odd, g_own, g_other),
        weight_grad.reshape(weight.shape),
    )


def solution(mesh):
    rows, cols = (mesh.shape["rows"], mesh.shape["cols"])
    fine = Mesh(mesh.devices.reshape(rows, cols // 2, 2), ("rows",) + COLS)
    placed = P("rows", COLS, None)
    return jax.shard_map(
        body,
        mesh=fine,
        in_specs=(placed, P(), placed),
        out_specs=(placed, placed, P()),
        check_vma=False,
    )
```

```python
import functools
import math

import jax
import jax.numpy as jnp
from jax import lax
from jax.experimental import pallas as pl
from jax.experimental.pallas import tpu as pltpu
from jax.sharding import Mesh
from jax.sharding import PartitionSpec as P

DILATION_STEP = 12
STRIP = 16
TOP = 14
COLS = ("x", "core")
CHIPS = ("rows", "x")
VMEM = pltpu.VMEM


def slots(odd):
    return (1 + odd, 2 - odd, 3 * (1 - odd), 3 * odd)


def gather_map(odd, blocks, left, right, ext):
    width = blocks[0].shape[1]
    for place, (block, slot) in enumerate(zip(blocks, slots(odd))):
        ext[slot, :, pl.ds(STRIP, width), :] = block[...]
        ext[slot, :, pl.ds(0, STRIP), :] = left[place]
        ext[slot, :, pl.ds(STRIP + width, STRIP), :] = right[place]


def shift_columns(ext, shifted, width):
    cout = ext.shape[3]
    for slot in range(4):
        whole = ext[slot].astype(jnp.float32)
        for q in range(3):
            start = STRIP + DILATION_STEP * (q - 1)
            shifted[slot, :, :, pl.ds(q * cout, cout)] = whole[:, start : start + width].astype(jnp.bfloat16)


def kernel_grad(par, f_own, f_par, d_own, d_par, d_near, d_far, left, right, keep, give, shifted, ext, acc):
    odd, core = (par[0], par[1])
    half, width, cout = d_own.shape
    cin = f_own.shape[2]
    pixels = half * width
    gather_map(odd, (d_own, d_par, d_near, d_far), left, right, ext)
    shift_columns(ext, shifted, width)
    own, partner = slots(odd)[:2]
    total = None
    for block, slot in ((f_own, own), (f_par, partner)):
        lhs = block[...].reshape(pixels, cin)
        rhs = jnp.concatenate([shifted[slot + 1 - a].reshape(pixels, 3 * cout) for a in range(3)], axis=1)
        term = lax.dot_general(lhs, rhs, (((0,), (0,)), ((), ())), preferred_element_type=jnp.float32)
        total = term if total is None else total + term
    for a in range(3):
        for b in range(3):
            start = (3 * a + 2 - b) * cout
            acc[pl.ds((3 * a + b) * cin, cin), :] = total[:, start : start + cout]
    size = keep.shape[0]
    keep[...] = acc[pl.ds(core * size, size), :]
    give[...] = acc[pl.ds((1 - core) * size, size), :]


def kernel_scale(chunk, par, keep, given, out):
    total = keep[...] + given[...]
    size, cout = keep.shape
    top = jnp.max(jnp.abs(total).reshape(size // 8, 8, cout), axis=0)
    most = jnp.max(jnp.max(top, axis=0, keepdims=True), axis=1, keepdims=True)
    level = jnp.ceil(jnp.log2(jnp.maximum(jnp.broadcast_to(most, (8, cout)), 2.0**-110)))
    scaled = total * jnp.exp2(TOP - level)[:1]
    for c in range(out.shape[0]):
        out[c, pl.ds(0, chunk), :] = scaled[c * chunk : (c + 1) * chunk]
        out[c, pl.ds(chunk, out.shape[1] - chunk), :] = jnp.broadcast_to(level[:1], (out.shape[1] - chunk, cout))


def kernel_sum(chunk, par, got, out):
    chips, deep, cout = got.shape
    levels = [got[i, pl.ds(chunk, 1), :] for i in range(chips)]
    highest = functools.reduce(jnp.maximum, levels)
    total = None
    for i in range(chips):
        term = got[i, pl.ds(0, chunk), :] * jnp.exp2(levels[i] - highest)
        total = term if total is None else total + term
    out[pl.ds(0, chunk), :] = total * (1.0 / chips)
    out[pl.ds(chunk, deep - chunk), :] = jnp.broadcast_to(highest, (deep - chunk, cout))


def kernel_back(par, w, shifted, out_own, out_par):
    odd = par[0]
    half, width, cin = out_own.shape
    pixels, depth = (half * width, shifted.shape[3])
    own, partner = slots(odd)[:2]
    for out, slot in ((out_own, own), (out_par, partner)):
        total = None
        for a in range(3):
            lhs = shifted[slot + 1 - a].reshape(pixels, depth)
            rhs = jnp.concatenate([w[a, 2 - q] for q in range(3)], axis=1)
            term = lax.dot_general(lhs, rhs, (((1,), (1,)), ((), ())), preferred_element_type=jnp.float32)
            total = term if total is None else total + term
        out[...] = total.astype(jnp.bfloat16).reshape(half, width, cin)


def kernel_out(par, w, f_own, f_par, f_near, f_far, left, right, out_own, out_par, ext):
    odd = par[0]
    half, width, cout = out_own.shape
    cin = f_own.shape[2]
    wide = width + 2 * STRIP
    gather_map(odd, (f_own, f_par, f_near, f_far), left, right, ext)
    own, partner = slots(odd)[:2]
    for out, slot in ((out_own, own), (out_par, partner)):
        total = None
        for a in range(3):
            lhs = ext[slot + a - 1].reshape(half * wide, cin)
            rhs = jnp.concatenate([w[a, b] for b in range(3)], axis=1)
            term = jnp.dot(lhs, rhs, preferred_element_type=jnp.float32)
            total = term if total is None else total + term
        total = total.reshape(half, wide, 3 * cout)
        result = None
        for b in range(3):
            start = STRIP + DILATION_STEP * (b - 1)
            term = total[:, start : start + width, b * cout : (b + 1) * cout]
            result = term if result is None else result + term
        out[...] = result.astype(jnp.bfloat16)


def call(kernel, operands, outs, scratch, flops):
    whole = pl.BlockSpec(memory_space=VMEM)
    size = sum(x.size * x.dtype.itemsize for x in operands) + sum(math.prod(o.shape) * o.dtype.itemsize for o in outs)
    return pl.pallas_call(
        kernel,
        out_shape=outs,
        in_specs=[pl.BlockSpec(memory_space=pltpu.SMEM)] + [whole] * (len(operands) - 1),
        out_specs=[whole] * len(outs),
        scratch_shapes=scratch,
        compiler_params=pltpu.CompilerParams(vmem_limit_bytes=12 * 1024 * 1024),
        cost_estimate=pl.CostEstimate(flops=flops, bytes_accessed=size if flops else 0, transcendentals=0),
    )(*operands)


def kernel_edges(par, *refs):
    blocks, (tails, heads) = (refs[:-2], refs[-2:])
    for place, block in enumerate(blocks):
        tails[place] = block[:, pl.ds(block.shape[1] - STRIP, STRIP), :]
        heads[place] = block[:, pl.ds(0, STRIP), :]


def edges(par, blocks, flops):
    half, _, depth = blocks[0].shape
    strip = jax.ShapeDtypeStruct((len(blocks), half, STRIP, depth), jnp.bfloat16)
    return call(kernel_edges, (par,) + blocks, [strip, strip], [], flops)


def exchanged(tails, heads, count):
    left = lax.ppermute(tails, COLS, [(i, i + 1) for i in range(count - 1)])
    right = lax.ppermute(heads, COLS, [(i + 1, i) for i in range(count - 1)])
    return left, right


def joined(odd, own, other):
    low = jnp.where(odd == 1, other, own)
    high = jnp.where(odd == 1, own, other)
    return jnp.concatenate([low, high], axis=0)


def body(features, weight, cotangent):
    height, width, cin = features.shape
    cout = weight.shape[3]
    half = height // 2
    rows = lax.axis_size("rows")
    cols = lax.axis_size("x") * lax.axis_size("core")
    chips = rows * lax.axis_size("x")
    odd = lax.axis_index("rows") % 2
    core = lax.axis_index("core")
    par = jnp.stack([odd, core]).astype(jnp.int32)

    swap = [(i, i ^ 1) for i in range(rows)]
    other_core = [(0, 1), (1, 0)]
    up = [(i, i + 2 if i % 2 else i - 2) for i in range(rows)]
    near = [(i, j) for i, j in up if 0 <= j < rows]
    far = [(j, i) for i, j in near]
    fence = lax.optimization_barrier

    def pick(cells, which):
        return lax.dynamic_slice_in_dim(cells, which * half, half, 0)

    wide = width + 2 * STRIP
    share = 9 * cin // 2
    chunk = share // chips
    deep = -(-(chunk + 1) // STRIP) * STRIP
    flops = 2 * 9 * height * width * cin * cout

    d_own, d_give = (pick(cotangent, odd), pick(cotangent, 1 - odd))
    f_own, f_give = (pick(features, odd), pick(features, 1 - odd))
    d_par = lax.ppermute(d_give, "rows", swap)
    d_near = lax.ppermute(d_own, "rows", near)
    f_par = lax.ppermute(f_give, "rows", swap)
    d_far = lax.ppermute(d_par, "rows", far)
    f_first, d_far = fence((f_own, d_far))
    f_near = lax.ppermute(f_first, "rows", near)
    f_far = lax.ppermute(f_par, "rows", far)
    d_blocks = (d_own, d_par, d_near, d_far)
    f_blocks = (f_own, f_par, f_near, f_far)
    d_left, d_right = exchanged(*edges(par, d_blocks, flops), cols)

    part = jax.ShapeDtypeStruct((share, cout), jnp.float32)
    keep, give, shifted = call(
        kernel_grad,
        (par, f_own, f_par) + d_blocks + (d_left, d_right),
        [part, part, jax.ShapeDtypeStruct((4, half, width, 3 * cout), jnp.bfloat16)],
        [VMEM((4, half, wide, cout), jnp.bfloat16), VMEM((9 * cin, cout), jnp.float32)],
        30 * flops,
    )
    given = lax.ppermute(give, "core", other_core)
    f_tails, f_heads = edges(par, f_blocks, 2 * flops)
    given, f_tails, f_heads = fence((given, f_tails, f_heads))

    (scaled,) = call(
        functools.partial(kernel_scale, chunk),
        (par, keep, given),
        [jax.ShapeDtypeStruct((chips, deep, cout), jnp.float32)],
        [],
        0,
    )
    scaled, f_tails, f_heads = fence((scaled.astype(jnp.float16), f_tails, f_heads))
    got = lax.all_to_all(scaled, CHIPS, 0, 0)
    shifted, _ = fence((shifted, scaled))
    half_grad = jax.ShapeDtypeStruct((half, width, cin), jnp.bfloat16)
    g_own, g_par = call(
        kernel_back, (par, weight, shifted), [half_grad, half_grad], [], 0
    )
    g_other = lax.ppermute(g_par, "rows", swap)
    got, g_par = fence((got, g_par))

    f_left, f_right = exchanged(f_tails, f_heads, cols)

    (mine,) = call(
        functools.partial(kernel_sum, chunk),
        (par, got.astype(jnp.float32)),
        [jax.ShapeDtypeStruct((deep, cout), jnp.float32)],
        [],
        0,
    )
    mine = mine.astype(jnp.float16)
    f_left, f_right, copies = fence((f_left, f_right, jnp.broadcast_to(mine[None], (chips, deep, cout))))
    spread = lax.all_to_all(copies, CHIPS, 0, 0)
    other = lax.ppermute(spread, "core", other_core)

    half_out = jax.ShapeDtypeStruct((half, width, cout), jnp.bfloat16)
    o_own, o_par = call(
        kernel_out,
        (par, weight) + f_blocks + (f_left, f_right),
        [half_out, half_out],
        [VMEM((4, half, wide, cin), jnp.bfloat16)],
        0,
    )
    o_other = lax.ppermute(o_par, "rows", swap)

    norm = chips / jnp.sqrt(jnp.float32(height * width * chips * 2))

    def restored(low, high):
        picked = jnp.where(core == 0, low, high)
        factor = jnp.exp2(picked[:1, chunk : chunk + 1].astype(jnp.float32) - TOP) * norm
        return (picked[:, :chunk].astype(jnp.float32) * factor).reshape(share, cout)

    weight_grad = jnp.concatenate([restored(spread, other), restored(other, spread)], axis=0)
    return (
        joined(odd, o_own, o_other),
        joined(odd, g_own, g_other),
        weight_grad.reshape(weight.shape),
    )


def solution(mesh):
    rows, cols = (mesh.shape["rows"], mesh.shape["cols"])
    fine = Mesh(mesh.devices.reshape(rows, cols // 2, 2), ("rows",) + COLS)
    placed = P("rows", COLS, None)
    return jax.shard_map(
        body,
        mesh=fine,
        in_specs=(placed, P(), placed),
        out_specs=(placed, placed, P()),
        check_vma=False,
    )
```

```python
import functools
import math

import jax
import jax.numpy as jnp
from jax import lax
from jax.experimental import pallas as pl
from jax.experimental.pallas import tpu as pltpu
from jax.sharding import Mesh
from jax.sharding import PartitionSpec as P

DILATION_STEP = 12
STRIP = 16
TOP = 14
COLS = ("x", "core")
CHIPS = ("rows", "x")
VMEM = pltpu.VMEM


def slots(odd):
    return (1 + odd, 2 - odd, 3 * (1 - odd), 3 * odd)


def gather_map(odd, blocks, left, right, ext):
    width = blocks[0].shape[1]
    for place, (block, slot) in enumerate(zip(blocks, slots(odd))):
        ext[slot, :, pl.ds(STRIP, width), :] = block[...]
        ext[slot, :, pl.ds(0, STRIP), :] = left[place]
        ext[slot, :, pl.ds(STRIP + width, STRIP), :] = right[place]


def shift_columns(ext, shifted, width):
    cout = ext.shape[3]
    for slot in range(4):
        whole = ext[slot].astype(jnp.float32)
        for q in range(3):
            start = STRIP + DILATION_STEP * (q - 1)
            shifted[slot, :, :, pl.ds(q * cout, cout)] = whole[:, start : start + width].astype(jnp.bfloat16)


def kernel_grad(par, f_own, f_par, d_own, d_par, d_near, d_far, left, right, keep, give, ext, shifted, acc):
    odd, core = (par[0], par[1])
    half, width, cout = d_own.shape
    cin = f_own.shape[2]
    pixels = half * width
    gather_map(odd, (d_own, d_par, d_near, d_far), left, right, ext)
    shift_columns(ext, shifted, width)
    own, partner = slots(odd)[:2]
    total = None
    for block, slot in ((f_own, own), (f_par, partner)):
        lhs = block[...].reshape(pixels, cin)
        rhs = jnp.concatenate([shifted[slot + 1 - a].reshape(pixels, 3 * cout) for a in range(3)], axis=1)
        term = lax.dot_general(lhs, rhs, (((0,), (0,)), ((), ())), preferred_element_type=jnp.float32)
        total = term if total is None else total + term
    for a in range(3):
        for b in range(3):
            start = (3 * a + 2 - b) * cout
            acc[pl.ds((3 * a + b) * cin, cin), :] = total[:, start : start + cout]
    size = keep.shape[0]
    keep[...] = acc[pl.ds(core * size, size), :]
    give[...] = acc[pl.ds((1 - core) * size, size), :]


def kernel_scale(chunk, par, keep, given, out):
    total = keep[...] + given[...]
    size, cout = keep.shape
    top = jnp.max(jnp.abs(total).reshape(size // 8, 8, cout), axis=0)
    most = jnp.max(jnp.max(top, axis=0, keepdims=True), axis=1, keepdims=True)
    level = jnp.ceil(jnp.log2(jnp.maximum(jnp.broadcast_to(most, (8, cout)), 2.0**-110)))
    scaled = total * jnp.exp2(TOP - level)[:1]
    for c in range(out.shape[0]):
        out[c, pl.ds(0, chunk), :] = scaled[c * chunk : (c + 1) * chunk]
        out[c, pl.ds(chunk, out.shape[1] - chunk), :] = jnp.broadcast_to(level[:1], (out.shape[1] - chunk, cout))


def kernel_sum(chunk, par, got, out):
    chips, deep, cout = got.shape
    levels = [got[i, pl.ds(chunk, 1), :] for i in range(chips)]
    highest = functools.reduce(jnp.maximum, levels)
    total = None
    for i in range(chips):
        term = got[i, pl.ds(0, chunk), :] * jnp.exp2(levels[i] - highest)
        total = term if total is None else total + term
    out[pl.ds(0, chunk), :] = total * (1.0 / chips)
    out[pl.ds(chunk, deep - chunk), :] = jnp.broadcast_to(highest, (deep - chunk, cout))


def kernel_back(par, d_own, d_par, d_near, d_far, w, left, right, out_own, out_par, ext, shifted, sems):
    odd = par[0]
    half, width, cout = d_own.shape
    cin = w.shape[2]
    pixels = half * width
    moves = []
    for place, (block, slot) in enumerate(zip((d_own, d_par, d_near, d_far), slots(odd))):
        move = pltpu.make_async_copy(block, ext.at[slot, :, pl.ds(STRIP, width), :], sems.at[place])
        move.start()
        moves.append(move)
        ext[slot, :, pl.ds(0, STRIP), :] = left[place]
        ext[slot, :, pl.ds(STRIP + width, STRIP), :] = right[place]
    for move in moves:
        move.wait()
    shift_columns(ext, shifted, width)
    own, partner = slots(odd)[:2]
    for out, slot in ((out_own, own), (out_par, partner)):
        total = None
        for a in range(3):
            lhs = shifted[slot + 1 - a].reshape(pixels, 3 * cout)
            rhs = jnp.concatenate([w[a, 2 - q] for q in range(3)], axis=1)
            term = lax.dot_general(lhs, rhs, (((1,), (1,)), ((), ())), preferred_element_type=jnp.float32)
            total = term if total is None else total + term
        out[...] = total.astype(jnp.bfloat16).reshape(half, width, cin)


def kernel_out(par, w, f_own, f_par, f_near, f_far, left, right, out_own, out_par, ext):
    odd = par[0]
    half, width, cout = out_own.shape
    cin = f_own.shape[2]
    wide = width + 2 * STRIP
    gather_map(odd, (f_own, f_par, f_near, f_far), left, right, ext)
    own, partner = slots(odd)[:2]
    for out, slot in ((out_own, own), (out_par, partner)):
        total = None
        for a in range(3):
            lhs = ext[slot + a - 1].reshape(half * wide, cin)
            rhs = jnp.concatenate([w[a, b] for b in range(3)], axis=1)
            term = jnp.dot(lhs, rhs, preferred_element_type=jnp.float32)
            total = term if total is None else total + term
        total = total.reshape(half, wide, 3 * cout)
        result = None
        for b in range(3):
            start = STRIP + DILATION_STEP * (b - 1)
            term = total[:, start : start + width, b * cout : (b + 1) * cout]
            result = term if result is None else result + term
        out[...] = result.astype(jnp.bfloat16)


def call(kernel, operands, outs, scratch, flops, outside=0):
    whole = pl.BlockSpec(memory_space=VMEM)
    size = sum(x.size * x.dtype.itemsize for x in operands) + sum(math.prod(o.shape) * o.dtype.itemsize for o in outs)
    return pl.pallas_call(
        kernel,
        out_shape=outs,
        in_specs=[pl.BlockSpec(memory_space=pltpu.SMEM)] + [pl.BlockSpec(memory_space=pl.ANY)] * outside
        + [whole] * (len(operands) - 1 - outside),
        out_specs=[whole] * len(outs),
        scratch_shapes=scratch,
        compiler_params=pltpu.CompilerParams(vmem_limit_bytes=12 * 1024 * 1024),
        cost_estimate=pl.CostEstimate(flops=flops, bytes_accessed=size if flops else 0, transcendentals=0),
    )(*operands)


def kernel_edges(par, *refs):
    blocks, (tails, heads) = (refs[:-2], refs[-2:])
    for place, block in enumerate(blocks):
        tails[place] = block[:, pl.ds(block.shape[1] - STRIP, STRIP), :]
        heads[place] = block[:, pl.ds(0, STRIP), :]


def packed(par, blocks, flops):
    half, _, depth = blocks[0].shape
    strip = jax.ShapeDtypeStruct((len(blocks), half, STRIP, depth), jnp.bfloat16)
    return call(kernel_edges, (par,) + blocks, [strip, strip], [], flops)


def edges(blocks):
    width = blocks[0].shape[1]
    tails = jnp.stack([x[:, width - STRIP :] for x in blocks])
    heads = jnp.stack([x[:, :STRIP] for x in blocks])
    return tails, heads


def exchanged(tails, heads, count):
    left = lax.ppermute(tails, COLS, [(i, i + 1) for i in range(count - 1)])
    right = lax.ppermute(heads, COLS, [(i + 1, i) for i in range(count - 1)])
    return left, right


def joined(odd, own, other):
    low = jnp.where(odd == 1, other, own)
    high = jnp.where(odd == 1, own, other)
    return jnp.concatenate([low, high], axis=0)


def body(features, weight, cotangent):
    height, width, cin = features.shape
    cout = weight.shape[3]
    half = height // 2
    rows = lax.axis_size("rows")
    cols = lax.axis_size("x") * lax.axis_size("core")
    chips = rows * lax.axis_size("x")
    odd = lax.axis_index("rows") % 2
    core = lax.axis_index("core")
    par = jnp.stack([odd, core]).astype(jnp.int32)

    swap = [(i, i ^ 1) for i in range(rows)]
    other_core = [(0, 1), (1, 0)]
    up = [(i, i + 2 if i % 2 else i - 2) for i in range(rows)]
    near = [(i, j) for i, j in up if 0 <= j < rows]
    far = [(j, i) for i, j in near]
    fence = lax.optimization_barrier

    def pick(cells, which):
        return lax.dynamic_slice_in_dim(cells, which * half, half, 0)

    wide = width + 2 * STRIP
    share = 9 * cin // 2
    chunk = share // chips
    deep = -(-(chunk + 1) // STRIP) * STRIP
    flops = 2 * 9 * height * width * cin * cout

    d_own, d_give = (pick(cotangent, odd), pick(cotangent, 1 - odd))
    f_own, f_give = (pick(features, odd), pick(features, 1 - odd))
    d_par = lax.ppermute(d_give, "rows", swap)
    d_near = lax.ppermute(d_own, "rows", near)
    f_par = lax.ppermute(f_give, "rows", swap)
    f_first, d_par, d_near = fence((f_own, d_par, d_near))
    d_far = lax.ppermute(d_par, "rows", far)
    f_near = lax.ppermute(f_first, "rows", near)
    f_far = lax.ppermute(f_par, "rows", far)
    d_blocks = (d_own, d_par, d_near, d_far)
    f_own, f_near = fence((f_own, f_near))
    d_left, d_right = exchanged(*packed(par, d_blocks, flops), cols)

    f_blocks = (f_own, f_par, f_near, f_far)
    part = jax.ShapeDtypeStruct((share, cout), jnp.float32)
    d_maps = [VMEM((4, half, wide, cout), jnp.bfloat16), VMEM((4, half, width, 3 * cout), jnp.bfloat16)]
    keep, give = call(
        kernel_grad,
        (par, f_own, f_par) + d_blocks + (d_left, d_right),
        [part, part],
        d_maps + [VMEM((9 * cin, cout), jnp.float32)],
        30 * flops,
    )
    given = lax.ppermute(give, "core", other_core)
    f_tails, f_heads = edges(f_blocks)
    given, f_tails, f_heads = fence((given, f_tails, f_heads))

    (scaled,) = call(
        functools.partial(kernel_scale, chunk),
        (par, keep, given),
        [jax.ShapeDtypeStruct((chips, deep, cout), jnp.float32)],
        [],
        0,
    )
    scaled, f_tails, f_heads = fence((scaled.astype(jnp.float16), f_tails, f_heads))
    got = lax.all_to_all(scaled, CHIPS, 0, 0)
    d_left, _ = fence((d_left, scaled))
    half_grad = jax.ShapeDtypeStruct((half, width, cin), jnp.bfloat16)
    g_own, g_par = call(
        kernel_back,
        (par,) + d_blocks + (weight, d_left, d_right),
        [half_grad, half_grad],
        d_maps + [pltpu.SemaphoreType.DMA((4,))],
        0,
        outside=4,
    )
    g_other = lax.ppermute(g_par, "rows", swap)
    got, g_par = fence((got, g_par))

    f_left, f_right = exchanged(f_tails, f_heads, cols)

    (mine,) = call(
        functools.partial(kernel_sum, chunk),
        (par, got.astype(jnp.float32)),
        [jax.ShapeDtypeStruct((deep, cout), jnp.float32)],
        [],
        0,
    )
    mine = mine.astype(jnp.float16)
    f_left, f_right, copies = fence((f_left, f_right, jnp.broadcast_to(mine[None], (chips, deep, cout))))
    spread = lax.all_to_all(copies, CHIPS, 0, 0)
    other = lax.ppermute(spread, "core", other_core)

    half_out = jax.ShapeDtypeStruct((half, width, cout), jnp.bfloat16)
    o_own, o_par = call(
        kernel_out,
        (par, weight) + f_blocks + (f_left, f_right),
        [half_out, half_out],
        [VMEM((4, half, wide, cin), jnp.bfloat16)],
        0,
    )
    o_other = lax.ppermute(o_par, "rows", swap)

    norm = chips / jnp.sqrt(jnp.float32(height * width * chips * 2))

    def restored(low, high):
        picked = jnp.where(core == 0, low, high)
        factor = jnp.exp2(picked[:1, chunk : chunk + 1].astype(jnp.float32) - TOP) * norm
        return (picked[:, :chunk].astype(jnp.float32) * factor).reshape(share, cout)

    weight_grad = jnp.concatenate([restored(spread, other), restored(other, spread)], axis=0)
    return (
        joined(odd, o_own, o_other),
        joined(odd, g_own, g_other),
        weight_grad.reshape(weight.shape),
    )


def solution(mesh):
    rows, cols = (mesh.shape["rows"], mesh.shape["cols"])
    fine = Mesh(mesh.devices.reshape(rows, cols // 2, 2), ("rows",) + COLS)
    placed = P("rows", COLS, None)
    return jax.shard_map(
        body,
        mesh=fine,
        in_specs=(placed, P(), placed),
        out_specs=(placed, placed, P()),
        check_vma=False,
    )
```

```python
import functools
import math

import jax
import jax.numpy as jnp
from jax import lax
from jax.experimental import pallas as pl
from jax.experimental.pallas import tpu as pltpu
from jax.sharding import Mesh
from jax.sharding import PartitionSpec as P

DILATION_STEP = 12
STRIP = 16
TOP = 14
COLS = ("x", "core")
CHIPS = ("rows", "x")
VMEM = pltpu.VMEM


def slots(odd):
    return (1 + odd, 2 - odd, 3 * (1 - odd), 3 * odd)


def gather_map(odd, blocks, left, right, ext):
    width = blocks[0].shape[1]
    for place, (block, slot) in enumerate(zip(blocks, slots(odd))):
        ext[slot, :, pl.ds(STRIP, width), :] = block[...]
        ext[slot, :, pl.ds(0, STRIP), :] = left[place]
        ext[slot, :, pl.ds(STRIP + width, STRIP), :] = right[place]


def shift_columns(ext, shifted, width):
    cout = ext.shape[3]
    for slot in range(4):
        whole = ext[slot].astype(jnp.float32)
        for q in range(3):
            start = STRIP + DILATION_STEP * (q - 1)
            shifted[slot, :, :, pl.ds(q * cout, cout)] = whole[:, start : start + width].astype(jnp.bfloat16)


def kernel_grad(par, f_own, f_par, d_own, d_par, d_near, d_far, left, right, keep, give, ext, shifted, acc):
    odd, core = (par[0], par[1])
    half, width, cout = d_own.shape
    cin = f_own.shape[2]
    pixels = half * width
    gather_map(odd, (d_own, d_par, d_near, d_far), left, right, ext)
    shift_columns(ext, shifted, width)
    own, partner = slots(odd)[:2]
    total = None
    for block, slot in ((f_own, own), (f_par, partner)):
        lhs = block[...].reshape(pixels, cin)
        rhs = jnp.concatenate([shifted[slot + 1 - a].reshape(pixels, 3 * cout) for a in range(3)], axis=1)
        term = lax.dot_general(lhs, rhs, (((0,), (0,)), ((), ())), preferred_element_type=jnp.float32)
        total = term if total is None else total + term
    for a in range(3):
        for b in range(3):
            start = (3 * a + 2 - b) * cout
            acc[pl.ds((3 * a + b) * cin, cin), :] = total[:, start : start + cout]
    size = keep.shape[0]
    keep[...] = acc[pl.ds(core * size, size), :]
    give[...] = acc[pl.ds((1 - core) * size, size), :]


def kernel_scale(chunk, par, keep, given, out):
    total = keep[...] + given[...]
    size, cout = keep.shape
    top = jnp.max(jnp.abs(total).reshape(size // 8, 8, cout), axis=0)
    most = jnp.max(jnp.max(top, axis=0, keepdims=True), axis=1, keepdims=True)
    level = jnp.ceil(jnp.log2(jnp.maximum(jnp.broadcast_to(most, (8, cout)), 2.0**-110)))
    scaled = total * jnp.exp2(TOP - level)[:1]
    for c in range(out.shape[0]):
        out[c, pl.ds(0, chunk), :] = scaled[c * chunk : (c + 1) * chunk]
        out[c, pl.ds(chunk, out.shape[1] - chunk), :] = jnp.broadcast_to(level[:1], (out.shape[1] - chunk, cout))


def kernel_sum(chunk, par, got, out):
    chips, deep, cout = got.shape
    levels = [got[i, pl.ds(chunk, 1), :] for i in range(chips)]
    highest = functools.reduce(jnp.maximum, levels)
    total = None
    for i in range(chips):
        term = got[i, pl.ds(0, chunk), :] * jnp.exp2(levels[i] - highest)
        total = term if total is None else total + term
    out[pl.ds(0, chunk), :] = total * (1.0 / chips)
    out[pl.ds(chunk, deep - chunk), :] = jnp.broadcast_to(highest, (deep - chunk, cout))


def kernel_back(par, w, d_own, d_par, d_near, d_far, left, right, out_own, out_par, ext, shifted):
    odd = par[0]
    half, width, cout = d_own.shape
    cin = w.shape[2]
    pixels = half * width
    gather_map(odd, (d_own, d_par, d_near, d_far), left, right, ext)
    shift_columns(ext, shifted, width)
    own, partner = slots(odd)[:2]
    for out, slot in ((out_own, own), (out_par, partner)):
        total = None
        for a in range(3):
            lhs = shifted[slot + 1 - a].reshape(pixels, 3 * cout)
            rhs = jnp.concatenate([w[a, 2 - q] for q in range(3)], axis=1)
            term = lax.dot_general(lhs, rhs, (((1,), (1,)), ((), ())), preferred_element_type=jnp.float32)
            total = term if total is None else total + term
        out[...] = total.astype(jnp.bfloat16).reshape(half, width, cin)


def kernel_out(par, w, f_own, f_par, f_near, f_far, left, right, out_own, out_par, ext):
    odd = par[0]
    half, width, cout = out_own.shape
    cin = f_own.shape[2]
    wide = width + 2 * STRIP
    gather_map(odd, (f_own, f_par, f_near, f_far), left, right, ext)
    own, partner = slots(odd)[:2]
    for out, slot in ((out_own, own), (out_par, partner)):
        total = None
        for a in range(3):
            lhs = ext[slot + a - 1].reshape(half * wide, cin)
            rhs = jnp.concatenate([w[a, b] for b in range(3)], axis=1)
            term = jnp.dot(lhs, rhs, preferred_element_type=jnp.float32)
            total = term if total is None else total + term
        total = total.reshape(half, wide, 3 * cout)
        result = None
        for b in range(3):
            start = STRIP + DILATION_STEP * (b - 1)
            term = total[:, start : start + width, b * cout : (b + 1) * cout]
            result = term if result is None else result + term
        out[...] = result.astype(jnp.bfloat16)


def call(kernel, operands, outs, scratch, flops):
    whole = pl.BlockSpec(memory_space=VMEM)
    size = sum(x.size * x.dtype.itemsize for x in operands) + sum(math.prod(o.shape) * o.dtype.itemsize for o in outs)
    return pl.pallas_call(
        kernel,
        out_shape=outs,
        in_specs=[pl.BlockSpec(memory_space=pltpu.SMEM)] + [whole] * (len(operands) - 1),
        out_specs=[whole] * len(outs),
        scratch_shapes=scratch,
        compiler_params=pltpu.CompilerParams(vmem_limit_bytes=12 * 1024 * 1024),
        cost_estimate=pl.CostEstimate(flops=flops, bytes_accessed=size if flops else 0, transcendentals=0),
    )(*operands)


def kernel_edges(par, *refs):
    blocks, (tails, heads) = (refs[:-2], refs[-2:])
    for place, block in enumerate(blocks):
        tails[place] = block[:, pl.ds(block.shape[1] - STRIP, STRIP), :]
        heads[place] = block[:, pl.ds(0, STRIP), :]


def packed(par, blocks, flops):
    half, _, depth = blocks[0].shape
    strip = jax.ShapeDtypeStruct((len(blocks), half, STRIP, depth), jnp.bfloat16)
    return call(kernel_edges, (par,) + blocks, [strip, strip], [], flops)


def edges(blocks):
    width = blocks[0].shape[1]
    tails = jnp.stack([x[:, width - STRIP :] for x in blocks])
    heads = jnp.stack([x[:, :STRIP] for x in blocks])
    return tails, heads


def exchanged(tails, heads, count):
    left = lax.ppermute(tails, COLS, [(i, i + 1) for i in range(count - 1)])
    right = lax.ppermute(heads, COLS, [(i + 1, i) for i in range(count - 1)])
    return left, right


def joined(odd, own, other):
    low = jnp.where(odd == 1, other, own)
    high = jnp.where(odd == 1, own, other)
    return jnp.concatenate([low, high], axis=0)


def body(features, weight, cotangent):
    height, width, cin = features.shape
    cout = weight.shape[3]
    half = height // 2
    rows = lax.axis_size("rows")
    cols = lax.axis_size("x") * lax.axis_size("core")
    chips = rows * lax.axis_size("x")
    odd = lax.axis_index("rows") % 2
    core = lax.axis_index("core")
    par = jnp.stack([odd, core]).astype(jnp.int32)

    swap = [(i, i ^ 1) for i in range(rows)]
    other_core = [(0, 1), (1, 0)]
    up = [(i, i + 2 if i % 2 else i - 2) for i in range(rows)]
    near = [(i, j) for i, j in up if 0 <= j < rows]
    far = [(j, i) for i, j in near]
    fence = lax.optimization_barrier

    def pick(cells, which):
        return lax.dynamic_slice_in_dim(cells, which * half, half, 0)

    wide = width + 2 * STRIP
    share = 9 * cin // 2
    chunk = share // chips
    deep = -(-(chunk + 1) // STRIP) * STRIP
    flops = 2 * 9 * height * width * cin * cout

    d_own, d_give = (pick(cotangent, odd), pick(cotangent, 1 - odd))
    f_own, f_give = (pick(features, odd), pick(features, 1 - odd))
    d_par = lax.ppermute(d_give, "rows", swap)
    d_near = lax.ppermute(d_own, "rows", near)
    f_par = lax.ppermute(f_give, "rows", swap)
    f_first, d_par, d_near = fence((f_own, d_par, d_near))
    d_far = lax.ppermute(d_par, "rows", far)
    f_near = lax.ppermute(f_first, "rows", near)
    f_far = lax.ppermute(f_par, "rows", far)
    d_blocks = (d_own, d_par, d_near, d_far)
    f_own, f_near = fence((f_own, f_near))
    d_left, d_right = exchanged(*packed(par, d_blocks, flops), cols)

    f_blocks = (f_own, f_par, f_near, f_far)
    part = jax.ShapeDtypeStruct((share, cout), jnp.float32)
    d_maps = [VMEM((4, half, wide, cout), jnp.bfloat16), VMEM((4, half, width, 3 * cout), jnp.bfloat16)]
    half_grad = jax.ShapeDtypeStruct((half, width, cin), jnp.bfloat16)
    g_own, g_par = call(
        kernel_back,
        (par, weight) + d_blocks + (d_left, d_right),
        [half_grad, half_grad],
        d_maps,
        30 * flops,
    )
    g_other = lax.ppermute(g_par, "rows", swap)
    f_own, g_par = fence((f_own, g_par))
    keep, give = call(
        kernel_grad,
        (par, f_own, f_par) + d_blocks + (d_left, d_right),
        [part, part],
        d_maps + [VMEM((9 * cin, cout), jnp.float32)],
        0,
    )
    given = lax.ppermute(give, "core", other_core)
    f_tails, f_heads = edges(f_blocks)
    given, f_tails, f_heads = fence((given, f_tails, f_heads))

    (scaled,) = call(
        functools.partial(kernel_scale, chunk),
        (par, keep, given),
        [jax.ShapeDtypeStruct((chips, deep, cout), jnp.float32)],
        [],
        0,
    )
    scaled, f_tails, f_heads = fence((scaled.astype(jnp.float16), f_tails, f_heads))
    got = lax.all_to_all(scaled, CHIPS, 0, 0)
    g_own, _ = fence((g_own, scaled))
    f_left, f_right = exchanged(f_tails, f_heads, cols)

    (mine,) = call(
        functools.partial(kernel_sum, chunk),
        (par, got.astype(jnp.float32)),
        [jax.ShapeDtypeStruct((deep, cout), jnp.float32)],
        [],
        0,
    )
    mine = mine.astype(jnp.float16)
    f_left, f_right, copies = fence((f_left, f_right, jnp.broadcast_to(mine[None], (chips, deep, cout))))
    spread = lax.all_to_all(copies, CHIPS, 0, 0)
    other = lax.ppermute(spread, "core", other_core)

    half_out = jax.ShapeDtypeStruct((half, width, cout), jnp.bfloat16)
    o_own, o_par = call(
        kernel_out,
        (par, weight) + f_blocks + (f_left, f_right),
        [half_out, half_out],
        [VMEM((4, half, wide, cin), jnp.bfloat16)],
        0,
    )
    o_other = lax.ppermute(o_par, "rows", swap)

    norm = chips / jnp.sqrt(jnp.float32(height * width * chips * 2))

    def restored(low, high):
        picked = jnp.where(core == 0, low, high)
        factor = jnp.exp2(picked[:1, chunk : chunk + 1].astype(jnp.float32) - TOP) * norm
        return (picked[:, :chunk].astype(jnp.float32) * factor).reshape(share, cout)

    weight_grad = jnp.concatenate([restored(spread, other), restored(other, spread)], axis=0)
    return (
        joined(odd, o_own, o_other),
        joined(odd, g_own, g_other),
        weight_grad.reshape(weight.shape),
    )


def solution(mesh):
    rows, cols = (mesh.shape["rows"], mesh.shape["cols"])
    fine = Mesh(mesh.devices.reshape(rows, cols // 2, 2), ("rows",) + COLS)
    placed = P("rows", COLS, None)
    return jax.shard_map(
        body,
        mesh=fine,
        in_specs=(placed, P(), placed),
        out_specs=(placed, placed, P()),
        check_vma=False,
    )
```

```python
import functools
import math

import jax
import jax.numpy as jnp
from jax import lax
from jax.experimental import pallas as pl
from jax.experimental.pallas import tpu as pltpu
from jax.sharding import Mesh
from jax.sharding import PartitionSpec as P

DILATION_STEP = 12
STRIP = 16
TOP = 14
COLS = ("x", "core")
CHIPS = ("rows", "x")
VMEM = pltpu.VMEM


def slots(odd):
    return (1 + odd, 2 - odd, 3 * (1 - odd), 3 * odd)


def gather_map(odd, blocks, left, right, ext):
    width = blocks[0].shape[1]
    for place, (block, slot) in enumerate(zip(blocks, slots(odd))):
        ext[slot, :, pl.ds(STRIP, width), :] = block[...]
        ext[slot, :, pl.ds(0, STRIP), :] = left[place]
        ext[slot, :, pl.ds(STRIP + width, STRIP), :] = right[place]


def shift_columns(ext, shifted, width):
    cout = ext.shape[3]
    for slot in range(4):
        whole = ext[slot].astype(jnp.float32)
        for q in range(3):
            start = STRIP + DILATION_STEP * (q - 1)
            shifted[slot, :, :, pl.ds(q * cout, cout)] = whole[:, start : start + width].astype(jnp.bfloat16)


def kernel_both(par, w, f_own, f_par, d_own, d_par, d_near, d_far, left, right, keep, give, g_own, g_par, ext, shifted, acc):
    odd, core = (par[0], par[1])
    half, width, cout = d_own.shape
    cin = f_own.shape[2]
    pixels = half * width
    gather_map(odd, (d_own, d_par, d_near, d_far), left, right, ext)
    shift_columns(ext, shifted, width)
    own, partner = slots(odd)[:2]
    total = None
    for block, slot in ((f_own, own), (f_par, partner)):
        lhs = block[...].reshape(pixels, cin)
        rhs = jnp.concatenate([shifted[slot + 1 - a].reshape(pixels, 3 * cout) for a in range(3)], axis=1)
        term = lax.dot_general(lhs, rhs, (((0,), (0,)), ((), ())), preferred_element_type=jnp.float32)
        total = term if total is None else total + term
    for a in range(3):
        for b in range(3):
            start = (3 * a + 2 - b) * cout
            acc[pl.ds((3 * a + b) * cin, cin), :] = total[:, start : start + cout]
    size = keep.shape[0]
    keep[...] = acc[pl.ds(core * size, size), :]
    give[...] = acc[pl.ds((1 - core) * size, size), :]
    for out, slot in ((g_own, own), (g_par, partner)):
        total = None
        for a in range(3):
            lhs = shifted[slot + 1 - a].reshape(pixels, 3 * cout)
            rhs = jnp.concatenate([w[a, 2 - q] for q in range(3)], axis=1)
            term = lax.dot_general(lhs, rhs, (((1,), (1,)), ((), ())), preferred_element_type=jnp.float32)
            total = term if total is None else total + term
        out[...] = total.astype(jnp.bfloat16).reshape(half, width, cin)


def kernel_scale(chunk, par, keep, given, out):
    total = keep[...] + given[...]
    size, cout = keep.shape
    top = jnp.max(jnp.abs(total).reshape(size // 8, 8, cout), axis=0)
    most = jnp.max(jnp.max(top, axis=0, keepdims=True), axis=1, keepdims=True)
    level = jnp.ceil(jnp.log2(jnp.maximum(jnp.broadcast_to(most, (8, cout)), 2.0**-110)))
    scaled = total * jnp.exp2(TOP - level)[:1]
    for c in range(out.shape[0]):
        out[c, pl.ds(0, chunk), :] = scaled[c * chunk : (c + 1) * chunk]
        out[c, pl.ds(chunk, out.shape[1] - chunk), :] = jnp.broadcast_to(level[:1], (out.shape[1] - chunk, cout))


def kernel_sum(chunk, par, got, out):
    chips, deep, cout = got.shape
    levels = [got[i, pl.ds(chunk, 1), :] for i in range(chips)]
    highest = functools.reduce(jnp.maximum, levels)
    total = None
    for i in range(chips):
        term = got[i, pl.ds(0, chunk), :] * jnp.exp2(levels[i] - highest)
        total = term if total is None else total + term
    out[pl.ds(0, chunk), :] = total * (1.0 / chips)
    out[pl.ds(chunk, deep - chunk), :] = jnp.broadcast_to(highest, (deep - chunk, cout))


def kernel_out(par, w, f_own, f_par, f_near, f_far, left, right, out_own, out_par, ext):
    odd = par[0]
    half, width, cout = out_own.shape
    cin = f_own.shape[2]
    wide = width + 2 * STRIP
    gather_map(odd, (f_own, f_par, f_near, f_far), left, right, ext)
    own, partner = slots(odd)[:2]
    for out, slot in ((out_own, own), (out_par, partner)):
        total = None
        for a in range(3):
            lhs = ext[slot + a - 1].reshape(half * wide, cin)
            rhs = jnp.concatenate([w[a, b] for b in range(3)], axis=1)
            term = jnp.dot(lhs, rhs, preferred_element_type=jnp.float32)
            total = term if total is None else total + term
        total = total.reshape(half, wide, 3 * cout)
        result = None
        for b in range(3):
            start = STRIP + DILATION_STEP * (b - 1)
            term = total[:, start : start + width, b * cout : (b + 1) * cout]
            result = term if result is None else result + term
        out[...] = result.astype(jnp.bfloat16)


def call(kernel, operands, outs, scratch, flops):
    whole = pl.BlockSpec(memory_space=VMEM)
    size = sum(x.size * x.dtype.itemsize for x in operands) + sum(math.prod(o.shape) * o.dtype.itemsize for o in outs)
    return pl.pallas_call(
        kernel,
        out_shape=outs,
        in_specs=[pl.BlockSpec(memory_space=pltpu.SMEM)] + [whole] * (len(operands) - 1),
        out_specs=[whole] * len(outs),
        scratch_shapes=scratch,
        compiler_params=pltpu.CompilerParams(vmem_limit_bytes=16 * 1024 * 1024),
        cost_estimate=pl.CostEstimate(flops=flops, bytes_accessed=size if flops else 0, transcendentals=0),
    )(*operands)


def kernel_edges(par, *refs):
    blocks, (tails, heads) = (refs[:-2], refs[-2:])
    for place, block in enumerate(blocks):
        tails[place] = block[:, pl.ds(block.shape[1] - STRIP, STRIP), :]
        heads[place] = block[:, pl.ds(0, STRIP), :]


def packed(par, blocks, flops):
    half, _, depth = blocks[0].shape
    strip = jax.ShapeDtypeStruct((len(blocks), half, STRIP, depth), jnp.bfloat16)
    return call(kernel_edges, (par,) + blocks, [strip, strip], [], flops)


def edges(blocks):
    width = blocks[0].shape[1]
    tails = jnp.stack([x[:, width - STRIP :] for x in blocks])
    heads = jnp.stack([x[:, :STRIP] for x in blocks])
    return tails, heads


def exchanged(tails, heads, count):
    left = lax.ppermute(tails, COLS, [(i, i + 1) for i in range(count - 1)])
    right = lax.ppermute(heads, COLS, [(i + 1, i) for i in range(count - 1)])
    return left, right


def joined(odd, own, other):
    low = jnp.where(odd == 1, other, own)
    high = jnp.where(odd == 1, own, other)
    return jnp.concatenate([low, high], axis=0)


def body(features, weight, cotangent):
    height, width, cin = features.shape
    cout = weight.shape[3]
    half = height // 2
    rows = lax.axis_size("rows")
    cols = lax.axis_size("x") * lax.axis_size("core")
    chips = rows * lax.axis_size("x")
    odd = lax.axis_index("rows") % 2
    core = lax.axis_index("core")
    par = jnp.stack([odd, core]).astype(jnp.int32)

    swap = [(i, i ^ 1) for i in range(rows)]
    other_core = [(0, 1), (1, 0)]
    up = [(i, i + 2 if i % 2 else i - 2) for i in range(rows)]
    near = [(i, j) for i, j in up if 0 <= j < rows]
    far = [(j, i) for i, j in near]
    fence = lax.optimization_barrier

    def pick(cells, which):
        return lax.dynamic_slice_in_dim(cells, which * half, half, 0)

    wide = width + 2 * STRIP
    share = 9 * cin // 2
    chunk = share // chips
    deep = -(-(chunk + 1) // STRIP) * STRIP
    flops = 2 * 9 * height * width * cin * cout

    d_own, d_give = (pick(cotangent, odd), pick(cotangent, 1 - odd))
    f_own, f_give = (pick(features, odd), pick(features, 1 - odd))
    d_par = lax.ppermute(d_give, "rows", swap)
    d_near = lax.ppermute(d_own, "rows", near)
    f_par = lax.ppermute(f_give, "rows", swap)
    f_first, d_par, d_near = fence((f_own, d_par, d_near))
    d_far = lax.ppermute(d_par, "rows", far)
    f_near = lax.ppermute(f_first, "rows", near)
    f_far = lax.ppermute(f_par, "rows", far)
    d_blocks = (d_own, d_par, d_near, d_far)
    f_own, f_near = fence((f_own, f_near))
    d_left, d_right = exchanged(*edges(d_blocks), cols)

    f_blocks = (f_own, f_par, f_near, f_far)
    part = jax.ShapeDtypeStruct((share, cout), jnp.float32)
    half_grad = jax.ShapeDtypeStruct((half, width, cin), jnp.bfloat16)
    keep, give, g_own, g_par = call(
        kernel_both,
        (par, weight, f_own, f_par) + d_blocks + (d_left, d_right),
        [part, part, half_grad, half_grad],
        [
            VMEM((4, half, wide, cout), jnp.bfloat16),
            VMEM((4, half, width, 3 * cout), jnp.bfloat16),
            VMEM((9 * cin, cout), jnp.float32),
        ],
        30 * flops,
    )
    g_other = lax.ppermute(g_par, "rows", swap)
    given = lax.ppermute(give, "core", other_core)
    f_tails, f_heads = edges(f_blocks)
    given, f_tails, f_heads = fence((given, f_tails, f_heads))

    (scaled,) = call(
        functools.partial(kernel_scale, chunk),
        (par, keep, given),
        [jax.ShapeDtypeStruct((chips, deep, cout), jnp.float32)],
        [],
        0,
    )
    scaled, f_tails, f_heads = fence((scaled.astype(jnp.float16), f_tails, f_heads))
    got = lax.all_to_all(scaled, CHIPS, 0, 0)
    g_own, _ = fence((g_own, scaled))
    f_left, f_right = exchanged(f_tails, f_heads, cols)

    (mine,) = call(
        functools.partial(kernel_sum, chunk),
        (par, got.astype(jnp.float32)),
        [jax.ShapeDtypeStruct((deep, cout), jnp.float32)],
        [],
        0,
    )
    mine = mine.astype(jnp.float16)
    f_left, f_right, copies = fence((f_left, f_right, jnp.broadcast_to(mine[None], (chips, deep, cout))))
    spread = lax.all_to_all(copies, CHIPS, 0, 0)
    other = lax.ppermute(spread, "core", other_core)

    half_out = jax.ShapeDtypeStruct((half, width, cout), jnp.bfloat16)
    o_own, o_par = call(
        kernel_out,
        (par, weight) + f_blocks + (f_left, f_right),
        [half_out, half_out],
        [VMEM((4, half, wide, cin), jnp.bfloat16)],
        0,
    )
    o_other = lax.ppermute(o_par, "rows", swap)

    norm = chips / jnp.sqrt(jnp.float32(height * width * chips * 2))

    def restored(low, high):
        picked = jnp.where(core == 0, low, high)
        factor = jnp.exp2(picked[:1, chunk : chunk + 1].astype(jnp.float32) - TOP) * norm
        return (picked[:, :chunk].astype(jnp.float32) * factor).reshape(share, cout)

    weight_grad = jnp.concatenate([restored(spread, other), restored(other, spread)], axis=0)
    return (
        joined(odd, o_own, o_other),
        joined(odd, g_own, g_other),
        weight_grad.reshape(weight.shape),
    )


def solution(mesh):
    rows, cols = (mesh.shape["rows"], mesh.shape["cols"])
    fine = Mesh(mesh.devices.reshape(rows, cols // 2, 2), ("rows",) + COLS)
    placed = P("rows", COLS, None)
    return jax.shard_map(
        body,
        mesh=fine,
        in_specs=(placed, P(), placed),
        out_specs=(placed, placed, P()),
        check_vma=False,
    )
```

```python
import functools
import math

import jax
import jax.numpy as jnp
from jax import lax
from jax.experimental import pallas as pl
from jax.experimental.pallas import tpu as pltpu
from jax.sharding import Mesh
from jax.sharding import PartitionSpec as P

DILATION_STEP = 12
STRIP = 16
TOP = 14
COLS = ("x", "core")
CHIPS = ("rows", "x")
VMEM = pltpu.VMEM


def slots(odd):
    return (1 + odd, 2 - odd, 3 * (1 - odd), 3 * odd)


def gather_map(odd, blocks, left, right, ext):
    width = blocks[0].shape[1]
    for place, (block, slot) in enumerate(zip(blocks, slots(odd))):
        ext[slot, :, pl.ds(STRIP, width), :] = block[...]
        ext[slot, :, pl.ds(0, STRIP), :] = left[place]
        ext[slot, :, pl.ds(STRIP + width, STRIP), :] = right[place]


def shift_columns(ext, shifted, width):
    cout = ext.shape[3]
    for slot in range(4):
        whole = ext[slot].astype(jnp.float32)
        for q in range(3):
            start = STRIP + DILATION_STEP * (q - 1)
            shifted[slot, :, :, pl.ds(q * cout, cout)] = whole[:, start : start + width].astype(jnp.bfloat16)


def kernel_both(par, w, f_own, f_par, d_own, d_par, d_near, d_far, left, right, keep, give, g_own, g_par, ext, shifted, acc):
    odd, core = (par[0], par[1])
    half, width, cout = d_own.shape
    cin = f_own.shape[2]
    pixels = half * width
    gather_map(odd, (d_own, d_par, d_near, d_far), left, right, ext)
    shift_columns(ext, shifted, width)
    own, partner = slots(odd)[:2]
    total = None
    for block, slot in ((f_own, own), (f_par, partner)):
        lhs = block[...].reshape(pixels, cin)
        rhs = jnp.concatenate([shifted[slot + 1 - a].reshape(pixels, 3 * cout) for a in range(3)], axis=1)
        term = lax.dot_general(lhs, rhs, (((0,), (0,)), ((), ())), preferred_element_type=jnp.float32)
        total = term if total is None else total + term
    for a in range(3):
        for b in range(3):
            start = (3 * a + 2 - b) * cout
            acc[pl.ds((3 * a + b) * cin, cin), :] = total[:, start : start + cout]
    size = keep.shape[0]
    keep[...] = acc[pl.ds(core * size, size), :]
    give[...] = acc[pl.ds((1 - core) * size, size), :]
    for out, slot in ((g_own, own), (g_par, partner)):
        total = None
        for a in range(3):
            lhs = shifted[slot + 1 - a].reshape(pixels, 3 * cout)
            rhs = jnp.concatenate([w[a, 2 - q] for q in range(3)], axis=1)
            term = lax.dot_general(lhs, rhs, (((1,), (1,)), ((), ())), preferred_element_type=jnp.float32)
            total = term if total is None else total + term
        out[...] = total.astype(jnp.bfloat16).reshape(half, width, cin)


def kernel_scale(chunk, par, keep, given, out):
    total = keep[...] + given[...]
    size, cout = keep.shape
    top = jnp.max(jnp.abs(total).reshape(size // 8, 8, cout), axis=0)
    most = jnp.max(jnp.max(top, axis=0, keepdims=True), axis=1, keepdims=True)
    level = jnp.ceil(jnp.log2(jnp.maximum(jnp.broadcast_to(most, (8, cout)), 2.0**-110)))
    scaled = total * jnp.exp2(TOP - level)[:1]
    for c in range(out.shape[0]):
        out[c, pl.ds(0, chunk), :] = scaled[c * chunk : (c + 1) * chunk]
        out[c, pl.ds(chunk, out.shape[1] - chunk), :] = jnp.broadcast_to(level[:1], (out.shape[1] - chunk, cout))


def kernel_sum(chunk, par, got, out):
    chips, deep, cout = got.shape
    levels = [got[i, pl.ds(chunk, 1), :] for i in range(chips)]
    highest = functools.reduce(jnp.maximum, levels)
    total = None
    for i in range(chips):
        term = got[i, pl.ds(0, chunk), :] * jnp.exp2(levels[i] - highest)
        total = term if total is None else total + term
    out[pl.ds(0, chunk), :] = total * (1.0 / chips)
    out[pl.ds(chunk, deep - chunk), :] = jnp.broadcast_to(highest, (deep - chunk, cout))


def kernel_out(par, w, f_own, f_par, f_near, f_far, left, right, out_own, out_par, ext):
    odd = par[0]
    half, width, cout = out_own.shape
    cin = f_own.shape[2]
    wide = width + 2 * STRIP
    gather_map(odd, (f_own, f_par, f_near, f_far), left, right, ext)
    own, partner = slots(odd)[:2]
    for out, slot in ((out_own, own), (out_par, partner)):
        total = None
        for a in range(3):
            lhs = ext[slot + a - 1].reshape(half * wide, cin)
            rhs = jnp.concatenate([w[a, b] for b in range(3)], axis=1)
            term = jnp.dot(lhs, rhs, preferred_element_type=jnp.float32)
            total = term if total is None else total + term
        total = total.reshape(half, wide, 3 * cout)
        result = None
        for b in range(3):
            start = STRIP + DILATION_STEP * (b - 1)
            term = total[:, start : start + width, b * cout : (b + 1) * cout]
            result = term if result is None else result + term
        out[...] = result.astype(jnp.bfloat16)


def call(kernel, operands, outs, scratch, flops):
    whole = pl.BlockSpec(memory_space=VMEM)
    size = sum(x.size * x.dtype.itemsize for x in operands) + sum(math.prod(o.shape) * o.dtype.itemsize for o in outs)
    return pl.pallas_call(
        kernel,
        out_shape=outs,
        in_specs=[pl.BlockSpec(memory_space=pltpu.SMEM)] + [whole] * (len(operands) - 1),
        out_specs=[whole] * len(outs),
        scratch_shapes=scratch,
        compiler_params=pltpu.CompilerParams(vmem_limit_bytes=16 * 1024 * 1024),
        cost_estimate=pl.CostEstimate(flops=flops, bytes_accessed=size if flops else 0, transcendentals=0),
    )(*operands)


def edges(blocks):
    width = blocks[0].shape[1]
    tails = jnp.stack([x[:, width - STRIP :] for x in blocks])
    heads = jnp.stack([x[:, :STRIP] for x in blocks])
    return tails, heads


def exchanged(tails, heads, count):
    left = lax.ppermute(tails, COLS, [(i, i + 1) for i in range(count - 1)])
    right = lax.ppermute(heads, COLS, [(i + 1, i) for i in range(count - 1)])
    return left, right


def paired(place, own, other):
    lead = lax.broadcasted_iota(jnp.int32, (2,) + (1,) * own.ndim, 0)
    return jnp.where(lead == place, own[None], other[None])


def body(features, weight, cotangent):
    height, width, cin = features.shape
    cout = weight.shape[3]
    half = height // 2
    rows = lax.axis_size("rows")
    cols = lax.axis_size("x") * lax.axis_size("core")
    chips = rows * lax.axis_size("x")
    odd = lax.axis_index("rows") % 2
    core = lax.axis_index("core")
    par = jnp.stack([odd, core]).astype(jnp.int32)

    swap = [(i, i ^ 1) for i in range(rows)]
    other_core = [(0, 1), (1, 0)]
    up = [(i, i + 2 if i % 2 else i - 2) for i in range(rows)]
    near = [(i, j) for i, j in up if 0 <= j < rows]
    far = [(j, i) for i, j in near]
    fence = lax.optimization_barrier

    def pick(cells, which):
        return lax.dynamic_slice_in_dim(cells, which * half, half, 0)

    wide = width + 2 * STRIP
    share = 9 * cin // 2
    chunk = share // chips
    deep = -(-(chunk + 1) // STRIP) * STRIP
    flops = 2 * 9 * height * width * cin * cout

    d_own, d_give = (pick(cotangent, odd), pick(cotangent, 1 - odd))
    f_own, f_give = (pick(features, odd), pick(features, 1 - odd))
    d_par = lax.ppermute(d_give, "rows", swap)
    d_near = lax.ppermute(d_own, "rows", near)
    f_par = lax.ppermute(f_give, "rows", swap)
    f_first, d_par, d_near = fence((f_own, d_par, d_near))
    d_far = lax.ppermute(d_par, "rows", far)
    f_near = lax.ppermute(f_first, "rows", near)
    f_far = lax.ppermute(f_par, "rows", far)
    d_blocks = (d_own, d_par, d_near, d_far)
    f_own, f_near = fence((f_own, f_near))
    d_left, d_right = exchanged(*edges(d_blocks), cols)

    f_blocks = (f_own, f_par, f_near, f_far)
    part = jax.ShapeDtypeStruct((share, cout), jnp.float32)
    half_grad = jax.ShapeDtypeStruct((half, width, cin), jnp.bfloat16)
    keep, give, g_own, g_par = call(
        kernel_both,
        (par, weight, f_own, f_par) + d_blocks + (d_left, d_right),
        [part, part, half_grad, half_grad],
        [
            VMEM((4, half, wide, cout), jnp.bfloat16),
            VMEM((4, half, width, 3 * cout), jnp.bfloat16),
            VMEM((9 * cin, cout), jnp.float32),
        ],
        30 * flops,
    )
    g_other = lax.ppermute(g_par, "rows", swap)
    given = lax.ppermute(give, "core", other_core)
    f_tails, f_heads = edges(f_blocks)
    given, f_tails, f_heads = fence((given, f_tails, f_heads))

    (scaled,) = call(
        functools.partial(kernel_scale, chunk),
        (par, keep, given),
        [jax.ShapeDtypeStruct((chips, deep, cout), jnp.float32)],
        [],
        0,
    )
    scaled, f_tails, f_heads = fence((scaled.astype(jnp.float16), f_tails, f_heads))
    got = lax.all_to_all(scaled, CHIPS, 0, 0)
    g_own, _ = fence((g_own, scaled))
    f_left, f_right = exchanged(f_tails, f_heads, cols)

    (mine,) = call(
        functools.partial(kernel_sum, chunk),
        (par, got.astype(jnp.float32)),
        [jax.ShapeDtypeStruct((deep, cout), jnp.float32)],
        [],
        0,
    )
    mine = mine.astype(jnp.float16)
    f_left, f_right, copies = fence((f_left, f_right, jnp.broadcast_to(mine[None], (chips, deep, cout))))
    spread = lax.all_to_all(copies, CHIPS, 0, 0)
    other = lax.ppermute(spread, "core", other_core)

    half_out = jax.ShapeDtypeStruct((half, width, cout), jnp.bfloat16)
    o_own, o_par = call(
        kernel_out,
        (par, weight) + f_blocks + (f_left, f_right),
        [half_out, half_out],
        [VMEM((4, half, wide, cin), jnp.bfloat16)],
        0,
    )
    o_other = lax.ppermute(o_par, "rows", swap)

    norm = chips / jnp.sqrt(jnp.float32(height * width * chips * 2))

    levels = paired(core, spread[:1, chunk : chunk + 1], other[:1, chunk : chunk + 1])
    factor = jnp.exp2(levels.astype(jnp.float32) - TOP) * norm
    weight_grad = paired(core, spread[:, :chunk], other[:, :chunk]).astype(jnp.float32) * factor
    return (
        paired(odd, o_own, o_other).reshape(height, width, cout),
        paired(odd, g_own, g_other).reshape(height, width, cin),
        weight_grad.reshape(weight.shape),
    )


def solution(mesh):
    rows, cols = (mesh.shape["rows"], mesh.shape["cols"])
    fine = Mesh(mesh.devices.reshape(rows, cols // 2, 2), ("rows",) + COLS)
    placed = P("rows", COLS, None)
    return jax.shard_map(
        body,
        mesh=fine,
        in_specs=(placed, P(), placed),
        out_specs=(placed, placed, P()),
        check_vma=False,
    )
```
